512 devices in a mesh: row: 64 (over x, z, core), col: 8 (over y).
Axes of the slice: x: 4, y: 8, z: 8, core: 2. Of those that a mesh axis runs over, the one named last changes fastest.
Arguments:
- features: bfloat16 [262144, 512], P(('row', 'col')), may hold values from -6 to 6
- factor: float32 [262144, 1024], P(('row', 'col')), may hold values from -0.03 to 0.03
- ip_weights: float32 [262144], P(('row', 'col')), may hold values from 0.1 to 30
- pivot_owner: int32 [256], replicated, may hold values from 0 to 511, as said below
- pivot_position: int32 [256], replicated, may hold values from 0 to 511, as said below
Outputs:
- new_columns: float32 [262144, 256], P(('row', 'col'))
- gram_rows: float32 [256, 1280], replicated
The draws below stay inside these ranges and needn't reach their ends.
Inputs may be any that keep to these rules, and one draw needn't show every extreme that they name: `pivot_owner`: each device owns at most 3 pivots, and some device owns exactly 3. `pivot_position`: pivots with the same owner have different positions.
All inputs are finite; a program needn't handle non-finite values.
Results may differ from the reference program's by a relative error of at most 0.0003.
Values may be sent and summed in bfloat16 or wider, within the bound.
A program may use at most 64 MiB of HBM per device.

```python
import math
import jax
import jax.numpy as jnp
from jax import lax

F = 512
R = 1024
B = 256
ROWS_DEV = 512
SAMPLES = 262144
PIV_MOST = 3
DEVICES = 512


def pivot_layout(key):
    base = jax.random.fold_in(key, 7)
    key_sizes, key_devices, key_perm, key_shift = jax.random.split(base, 4)
    least = max(1, PIV_MOST // 2)
    group_sizes = jax.random.randint(key_sizes, (B,), least, PIV_MOST + 1).at[0].set(PIV_MOST)
    group_ends = jnp.cumsum(group_sizes)
    pivot_index = jnp.arange(B)
    group_of = jnp.sum((group_ends[None, :] <= pivot_index[:, None]).astype(jnp.int32), axis=1)
    group_start = jnp.where(group_of > 0, group_ends[jnp.maximum(group_of - 1, 0)], 0)
    within = pivot_index - group_start
    devices_perm = jax.random.permutation(key_devices, DEVICES)
    owner_ids = devices_perm[group_of]
    row_perm = jax.random.permutation(key_perm, ROWS_DEV)
    shifts = jax.random.randint(key_shift, (B,), 0, ROWS_DEV)
    positions = row_perm[(within + shifts[group_of]) % ROWS_DEV]
    return (owner_ids.astype(jnp.int32), positions.astype(jnp.int32))


def draw_pivot_owner(key, part):
    return pivot_layout(key)[0]


def draw_pivot_position(key, part):
    return pivot_layout(key)[1]


def draw_ip_weights(key, part):
    base = jax.random.fold_in(key, 23)
    rising = 1.0 + 2.0 * jnp.arange(SAMPLES, dtype=jnp.float32) / max(SAMPLES - 1, 1)
    level = jnp.exp(jax.random.uniform(base, (SAMPLES,), jnp.float32, math.log(0.1), math.log(10.0)))
    return level * rising


def draw_features(key, part):
    base = jax.random.fold_in(key, 31)
    values = jnp.clip(jax.random.normal(base, (SAMPLES, F), jnp.float32), -6.0, 6.0)
    return values.astype(jnp.bfloat16)


def draw_factor(key, part):
    base = jax.random.fold_in(key, 41)
    spread = 0.01
    values = jnp.clip(spread * jax.random.normal(base, (SAMPLES, R), jnp.float32), -3.0 * spread, 3.0 * spread)
    return values


def setup_inputs(seed: int = 0) -> dict:
    keys = jax.random.split(jax.random.key(seed), 6)
    return {
        "features": draw_features(jax.random.fold_in(keys[5], 71), 0),
        "factor": draw_factor(jax.random.fold_in(keys[5], 71), 0),
        "ip_weights": draw_ip_weights(jax.random.fold_in(keys[5], 71), 0),
        "pivot_owner": draw_pivot_owner(jax.random.fold_in(keys[5], 71), 0),
        "pivot_position": draw_pivot_position(jax.random.fold_in(keys[5], 71), 0),
    }


kernel_rates = (0.25, 0.5, 1.0)
kernel_mixes = (0.5, 0.3, 0.2)

def kernel_of(left, right):
    cross_term = jnp.dot(left.astype(jnp.float32), right.T.astype(jnp.float32), preferred_element_type=jnp.float32)
    left_norms = jnp.sum(jnp.square(left.astype(jnp.float32)), axis=1)
    right_norms = jnp.sum(jnp.square(right.astype(jnp.float32)), axis=1)
    distance = left_norms[:, None] + right_norms[None, :] - 2.0 * cross_term
    total = jnp.zeros_like(distance)
    for rate, mixing in zip(kernel_rates, kernel_mixes):
        total = total + mixing * jnp.exp(-(rate / F) * distance)
    return total

def reference(features, factor, ip_weights, pivot_owner, pivot_position):
    chosen = (pivot_owner * ROWS_DEV + pivot_position).astype(jnp.int32)
    pivot_x = features[chosen]
    pivot_h = factor[chosen]
    residual = kernel_of(features, pivot_x) - jnp.dot(factor, pivot_h.T, precision=lax.Precision.HIGHEST)
    block = kernel_of(pivot_x, pivot_x) - jnp.dot(pivot_h, pivot_h.T, precision=lax.Precision.HIGHEST)
    lower_block = jnp.linalg.cholesky(block)
    new_columns = jax.scipy.linalg.solve_triangular(lower_block, residual.T, lower=True).T
    weighted = new_columns * ip_weights[:, None]
    left_part = jnp.dot(weighted.T, factor, precision=lax.Precision.HIGHEST)
    right_part = jnp.dot(weighted.T, new_columns, precision=lax.Precision.HIGHEST)
    gram_rows = jnp.concatenate([left_part, right_part], axis=1) / SAMPLES
    return (new_columns, gram_rows)
```

```python
import functools

import jax
import jax.numpy as jnp
from jax import lax
from jax.experimental import pallas as pl
from jax.experimental.pallas import tpu as pltpu
from jax.sharding import Mesh
from jax.sharding import PartitionSpec as P

MESH = pl.DeviceIdType.MESH
AXES = ("x", "z", "c", "y")
SIZES = {"x": 4, "z": 8, "c": 2, "y": 8}
F = 512
R = 1024
B = 256
SLOTS = 4
H_SCALE = 2.0**20
HIGHEST = lax.Precision.HIGHEST


def coord(axis):
    return lax.axis_index(axis)


def peer(**offsets):
    return tuple(
        lax.rem(coord(a) + offsets[a] % SIZES[a], SIZES[a]) if a in offsets else coord(a) for a in AXES
    )


class Copies:
    def __init__(self, send_sem, recv_sem):
        self.send_sem, self.recv_sem, self.used = send_sem, recv_sem, 0

    def start(self, src, dst, device):
        copy = pltpu.make_async_remote_copy(
            src_ref=src,
            dst_ref=dst,
            send_sem=self.send_sem.at[self.used],
            recv_sem=self.recv_sem.at[self.used],
            device_id=device,
            device_id_type=MESH,
        )
        self.used += 1
        copy.start()
        return copy


def greet(peers):
    barrier = pltpu.get_barrier_semaphore()
    for device in peers:
        pl.semaphore_signal(barrier, inc=1, device_id=device, device_id_type=MESH)
    return lambda: pl.semaphore_wait(barrier, len(peers))


X_PEERS = [dict(x=d) for d in range(1, 4)]
Y_PEERS = [dict(y=d) for d in range(1, 8)]
Z_PEERS = [dict(z=d) for d in range(1, 8)]
ZC_PEERS = [dict(z=d, c=e) for d in range(8) for e in range(2) if (d, e) != (0, 0)]
CORE = dict(c=1)


def gather_kernel(sx, sh, gx, gh, ox, oh, rx, rh, tx, th, ax, ah, bx, bh, yx, yh, fx, fh, send_sem, recv_sem):
    x, z, c, y = (coord(a) for a in AXES)
    copies = Copies(send_sem, recv_sem)
    everyone = [peer(**o) for o in ZC_PEERS + X_PEERS + Y_PEERS]
    greet(everyone)()

    here = z * 2 + c
    pending = []
    for o in ZC_PEERS:
        pending.append(copies.start(sx, rx.at[here], peer(**o)))
        pending.append(copies.start(sh, rh.at[here], peer(**o)))
    rx[here] = sx[...]
    rh[here] = sh[...]
    for copy in pending:
        copy.wait()

    tx[...] = jnp.dot(
        gx[...], rx[...].reshape(16 * 16, 128), preferred_element_type=jnp.float32
    ).astype(jnp.bfloat16).reshape(4, 16, 128)
    codes = rh[...].reshape(16 * 32, 128).astype(jnp.int32)
    high = (codes + 128) >> 8
    low = codes - high * 256
    high = high.astype(jnp.float32).astype(jnp.bfloat16)
    low = low.astype(jnp.float32).astype(jnp.bfloat16)
    picked = 256.0 * jnp.dot(gh[...], high, preferred_element_type=jnp.float32) + jnp.dot(
        gh[...], low, preferred_element_type=jnp.float32
    )
    th[...] = picked.astype(jnp.int32).astype(jnp.int16).reshape(4, 2, 16, 128)

    pending = []
    for i, o in enumerate(X_PEERS):
        device = peer(**o)
        pending.append(copies.start(tx.at[device[0]], ax.at[i], device))
        pending.append(copies.start(th.at[device[0]], ah.at[i], device))
    for copy in pending:
        copy.wait()
    total_x = tx[x].astype(jnp.float32)
    total_h = th[x].astype(jnp.int32)
    for i in range(3):
        total_x = total_x + ax[i].astype(jnp.float32)
        total_h = total_h + ah[i].astype(jnp.int32)
    bx[...] = total_x.astype(jnp.bfloat16)
    bh[...] = total_h.astype(jnp.int16)

    pending = []
    for i, o in enumerate(Y_PEERS):
        pending.append(copies.start(bx, yx.at[i], peer(**o)))
        pending.append(copies.start(bh, yh.at[i], peer(**o)))
    for copy in pending:
        copy.wait()
    for i in range(7):
        total_x = total_x + yx[i].astype(jnp.float32)
        total_h = total_h + yh[i].astype(jnp.int32)
    fx[c, x, z] = total_x.astype(jnp.bfloat16)
    fh[c, x, z] = total_h.astype(jnp.int16)

    pending = []
    for o in Z_PEERS:
        pending.append(copies.start(fx.at[c, x, z], fx.at[c, x, z], peer(**o)))
        pending.append(copies.start(fh.at[c, x, z], fh.at[c, x, z], peer(**o)))
    for copy in pending:
        copy.wait()

    sibling = peer(**CORE)
    pending = []
    for o in X_PEERS:
        pending.append(copies.start(fx.at[c, x], fx.at[c, x], peer(**o)))
        pending.append(copies.start(fh.at[c, x], fh.at[c, x], peer(**o)))
    across = [
        copies.start(fx.at[c, x], fx.at[c, x], sibling),
        copies.start(fh.at[c, x], fh.at[c, x], sibling),
    ]
    for i, o in enumerate(X_PEERS):
        source = lax.rem(x + 4 - o["x"], 4)
        pending[2 * i].wait_recv()
        across.append(copies.start(fx.at[c, source], fx.at[c, source], sibling))
        pending[2 * i + 1].wait_recv()
        across.append(copies.start(fh.at[c, source], fh.at[c, source], sibling))
    for copy in pending:
        copy.wait_send()
    for copy in across:
        copy.wait()
    for core in range(2):
        for xb in range(4):
            for zb in range(8):
                rows = pl.ds((zb * 2 + core) * 16, 16)
                ox[rows, pl.ds(xb * 128, 128)] = fx[core, xb, zb]
                for j in range(2):
                    oh[rows, pl.ds((xb * 2 + j) * 128, 128)] = fh[core, xb, zb, j]


def gather_pivots(slot_x, slot_h, pick_x, pick_h):
    count = 2 * (15 + 3 + 7 + 7 + 3 + 4)
    vmem = pl.BlockSpec(memory_space=pltpu.VMEM)
    bf16, i16 = jnp.bfloat16, jnp.int16
    return pl.pallas_call(
        gather_kernel,
        out_shape=(
            jax.ShapeDtypeStruct((B, F), bf16),
            jax.ShapeDtypeStruct((B, R), i16),
        ),
        in_specs=[vmem] * 4,
        out_specs=(vmem, vmem),
        scratch_shapes=[
            pltpu.VMEM((16, 16, 128), bf16),
            pltpu.VMEM((16, 32, 128), i16),
            pltpu.VMEM((4, 16, 128), bf16),
            pltpu.VMEM((4, 2, 16, 128), i16),
            pltpu.VMEM((3, 16, 128), bf16),
            pltpu.VMEM((3, 2, 16, 128), i16),
            pltpu.VMEM((16, 128), bf16),
            pltpu.VMEM((2, 16, 128), i16),
            pltpu.VMEM((7, 16, 128), bf16),
            pltpu.VMEM((7, 2, 16, 128), i16),
            pltpu.VMEM((2, 4, 8, 16, 128), bf16),
            pltpu.VMEM((2, 4, 8, 2, 16, 128), i16),
            pltpu.SemaphoreType.DMA((count,)),
            pltpu.SemaphoreType.DMA((count,)),
        ],
        compiler_params=pltpu.CompilerParams(
            collective_id=0, has_side_effects=True, vmem_limit_bytes=32 * 2**20
        ),
    )(slot_x, slot_h, pick_x, pick_h)


CHUNKS = ((0, 3), (3, 2))


def sum_kernel(m, out, cl, a1, xl, a2, zl, a3, yl, send_sem, recv_sem):
    x, z, c, y = (coord(a) for a in AXES)
    copies = Copies(send_sem, recv_sem)
    everyone = [peer(**o) for o in [CORE] + X_PEERS + Y_PEERS + Z_PEERS]
    greet(everyone)()
    sibling = peer(**CORE)

    def core_out(o, n):
        return [copies.start(m.at[pl.ds(5 * (1 - c) + o, n)], cl.at[pl.ds(o, n)], sibling)]

    def core_in(o, n):
        a1[o : o + n] = m[pl.ds(5 * c + o, n)] + cl[o : o + n]

    def x_out(o, n):
        return [
            copies.start(a1.at[pl.ds(o, n), peer(**p)[0]], xl.at[i, pl.ds(o, n)], peer(**p))
            for i, p in enumerate(X_PEERS)
        ]

    def x_in(o, n):
        a2[o : o + n] = a1[o : o + n, x] + xl[0, o : o + n] + xl[1, o : o + n] + xl[2, o : o + n]

    def z_out(o, n):
        return [
            copies.start(a2.at[pl.ds(o, n), peer(**p)[1]], zl.at[i, pl.ds(o, n)], peer(**p))
            for i, p in enumerate(Z_PEERS)
        ]

    def z_in(o, n):
        total = a2[o : o + n, z]
        for i in range(7):
            total = total + zl[i, o : o + n]
        a3[o : o + n] = total
        yl[y, o : o + n] = total

    def y_out(o, n):
        return [copies.start(a3.at[pl.ds(o, n)], yl.at[y, pl.ds(o, n)], peer(**p)) for p in Y_PEERS]

    def y_in(o, n):
        total = yl[0, o : o + n]
        for i in range(1, 8):
            total = total + yl[i, o : o + n]
        out[pl.ds(5 * c + o, n), x, z] = total

    def back(o, n, place, peers):
        block = out.at[(pl.ds(5 * c + o, n), *place)]
        return [copies.start(block, block, peer(**p)) for p in peers]

    stages = [
        (core_out, core_in),
        (x_out, x_in),
        (z_out, z_in),
        (y_out, y_in),
        (lambda o, n: back(o, n, (x, z), Z_PEERS), None),
        (lambda o, n: back(o, n, (x,), X_PEERS), None),
        (lambda o, n: back(o, n, (), [CORE]), None),
    ]
    flying = {chunk: stages[0][0](*chunk) for chunk in CHUNKS}
    for s in range(len(stages)):
        for chunk in CHUNKS:
            for copy in flying[chunk]:
                copy.wait()
            if stages[s][1] is not None:
                stages[s][1](*chunk)
            if s + 1 < len(stages):
                flying[chunk] = stages[s + 1][0](*chunk)


def sum_everywhere(m):
    count = len(CHUNKS) * (1 + 3 + 7 + 7 + 7 + 3 + 1)
    vmem = pl.BlockSpec(memory_space=pltpu.VMEM)
    f32 = jnp.float32
    return pl.pallas_call(
        sum_kernel,
        out_shape=jax.ShapeDtypeStruct((10, 4, 8, 8, 128), f32),
        in_specs=[vmem],
        out_specs=vmem,
        scratch_shapes=[
            pltpu.VMEM((5, 4, 8, 8, 128), f32),
            pltpu.VMEM((5, 4, 8, 8, 128), f32),
            pltpu.VMEM((3, 5, 8, 8, 128), f32),
            pltpu.VMEM((5, 8, 8, 128), f32),
            pltpu.VMEM((7, 5, 8, 128), f32),
            pltpu.VMEM((5, 8, 128), f32),
            pltpu.VMEM((8, 5, 8, 128), f32),
            pltpu.SemaphoreType.DMA((count,)),
            pltpu.SemaphoreType.DMA((count,)),
        ],
        compiler_params=pltpu.CompilerParams(
            collective_id=1, has_side_effects=True, vmem_limit_bytes=32 * 2**20
        ),
    )(m)


def kernel_of(left, right):
    cross_term = jnp.dot(left, right.T, preferred_element_type=jnp.float32)
    left_norms = jnp.sum(jnp.square(left.astype(jnp.float32)), axis=1)
    right_norms = jnp.sum(jnp.square(right.astype(jnp.float32)), axis=1)
    distance = left_norms[:, None] + right_norms[None, :] - 2.0 * cross_term
    quarter = jnp.exp(-(0.25 / F) * distance)
    half = quarter * quarter
    return 0.5 * quarter + 0.3 * half + 0.2 * (half * half)


def body(features, factor, ip_weights, pivot_owner, pivot_position):
    x, z, c, y = (coord(a) for a in AXES)
    me = ((x * 8 + z) * 2 + c) * 8 + y
    same_owner = pivot_owner[:, None] == pivot_owner[None, :]
    earlier = jnp.arange(B)[None, :] < jnp.arange(B)[:, None]
    rank = jnp.sum((same_owner & earlier).astype(jnp.int32), axis=1)
    chosen = (pivot_owner == me)[None, :] & (rank[None, :] == jnp.arange(SLOTS)[:, None])
    rows = jnp.sum(jnp.where(chosen, pivot_position[None, :], 0), axis=1)
    slot_x = features[rows].reshape(16, 128)
    slot_h = jnp.round(factor[rows] * H_SCALE).astype(jnp.int16).reshape(32, 128)

    first = (z * 2 + c) * 16
    owner = lax.dynamic_slice(pivot_owner, (first,), (16,))
    order = lax.dynamic_slice(rank, (first,), (16,))
    near = (owner // 128 == x) & (owner % 8 == y)
    line = (owner // 8) % 16
    row_x = jnp.where(near, line * 16 + order * 4, -64)
    row_h = jnp.where(near, line * 32 + order * 8, -64)
    pick_x = (
        (row_x[None, :] + jnp.arange(4)[:, None]).reshape(64, 1) == jnp.arange(256)[None, :]
    ).astype(jnp.bfloat16)
    pick_h = (
        (row_h[None, :] + jnp.arange(8)[:, None]).reshape(128, 1) == jnp.arange(512)[None, :]
    ).astype(jnp.bfloat16)
    pivot_x, pivot_h = gather_pivots(slot_x, slot_h, pick_x, pick_h)
    pivot_h = pivot_h.astype(jnp.float32) * (1.0 / H_SCALE)

    residual = kernel_of(features, pivot_x) - jnp.dot(factor, pivot_h.T, precision=HIGHEST)
    block = kernel_of(pivot_x, pivot_x) - jnp.dot(pivot_h, pivot_h.T, precision=HIGHEST)
    weighted = residual * ip_weights[:, None]
    local = jnp.dot(
        weighted.T, jnp.concatenate([factor, residual], axis=1), precision=HIGHEST
    )
    total = sum_everywhere(local.reshape(B, 10, 128).swapaxes(0, 1).reshape(10, 4, 8, 8, 128))
    total = total.reshape(10, B, 128).swapaxes(0, 1).reshape(B, 1280)

    lower = jnp.linalg.cholesky(block)
    inverse = jax.scipy.linalg.solve_triangular(lower, jnp.eye(B, dtype=jnp.float32), lower=True)
    new_columns = jnp.dot(residual, inverse.T, precision=HIGHEST)
    gram = jnp.dot(inverse, total, precision=HIGHEST)
    right = jnp.dot(gram[:, R:], inverse.T, precision=HIGHEST)
    gram = jnp.concatenate([gram[:, :R], right], axis=1)
    return (new_columns, gram / (512 * 512))


def solution(mesh):
    torus = Mesh(mesh.devices.reshape(4, 8, 2, 8), AXES)
    spread = P(AXES)
    in_specs = (P(AXES, None), P(AXES, None), spread, P(), P())
    out_specs = (P(AXES, None), P())
    return jax.shard_map(body, mesh=torus, in_specs=in_specs, out_specs=out_specs, check_vma=False)
```

```python
import jax
import jax.numpy as jnp
from jax import lax
from jax.experimental import pallas as pl
from jax.experimental.pallas import tpu as pltpu
from jax.sharding import Mesh
from jax.sharding import PartitionSpec as P

MESH = pl.DeviceIdType.MESH
AXES = ("x", "z", "c", "y")
SIZES = {"x": 4, "z": 8, "c": 2, "y": 8}
F = 512
R = 1024
B = 256
H_SCALE = 2.0**20


def coord(axis):
    return lax.axis_index(axis)


def peer(**offsets):
    return tuple(
        lax.rem(coord(a) + offsets[a] % SIZES[a], SIZES[a]) if a in offsets else coord(a) for a in AXES
    )


class Copies:
    def __init__(self, send_sem, recv_sem):
        self.send_sem, self.recv_sem, self.used = send_sem, recv_sem, 0

    def start(self, src, dst, device):
        copy = pltpu.make_async_remote_copy(
            src_ref=src,
            dst_ref=dst,
            send_sem=self.send_sem.at[self.used],
            recv_sem=self.recv_sem.at[self.used],
            device_id=device,
            device_id_type=MESH,
        )
        self.used += 1
        copy.start()
        return copy


def greet(peers):
    barrier = pltpu.get_barrier_semaphore()
    for device in peers:
        pl.semaphore_signal(barrier, inc=1, device_id=device, device_id_type=MESH)
    return lambda: pl.semaphore_wait(barrier, len(peers))


X_PEERS = [dict(x=d) for d in (1, 3, 2)]
Y_PEERS = [dict(y=d) for d in range(1, 8)]
Z_STEPS = (0, 1, 7, 2, 6, 3, 5, 4)
Z_PEERS = [dict(z=d) for d in Z_STEPS[1:]]
ZC_PEERS = [dict(z=d, c=e) for d in Z_STEPS for e in range(2) if (d, e) != (0, 0)]
CORE = dict(c=1)
Z_GROUPS = ((0, 5), (5, 3))


CHUNKS = ((0, 3), (3, 2))
W = 16


def split(values, count):
    out = []
    for _ in range(count - 1):
        part = values.astype(jnp.bfloat16)
        out.append(part)
        values = values - part.astype(jnp.float32)
    return out + [values.astype(jnp.bfloat16)]


def product(left, right, dims, count):
    order = {2: ((0, 0), (0, 1), (1, 0)), 3: ((0, 0), (0, 1), (1, 0), (0, 2), (2, 0), (1, 1))}[count]
    lhs = jnp.concatenate([left[i] for i, _ in order], axis=dims[0])
    rhs = jnp.concatenate([right[j] for _, j in order], axis=dims[1])
    return lax.dot_general(
        lhs, rhs, (((dims[0],), (dims[1],)), ((), ())), preferred_element_type=jnp.float32
    )


def row_norms(samples):
    ones = jnp.ones((8, F), jnp.bfloat16)
    norms = sum(
        lax.dot_general(ones, s, (((1,), (1,)), ((), ())), preferred_element_type=jnp.float32)
        for s in split(jnp.square(samples.astype(jnp.float32)), 2)
    )
    return norms[0:1]


def transposed_kernel(pivots, samples, norms):
    cross = lax.dot_general(
        pivots, samples, (((1,), (1,)), ((), ())), preferred_element_type=jnp.float32
    )
    pivot_norms = jnp.sum(jnp.square(pivots.astype(jnp.float32)), axis=1, keepdims=True)
    distance = pivot_norms + norms - 2.0 * cross
    quarter = jnp.exp(-(0.25 / F) * distance)
    half = quarter * quarter
    return 0.5 * quarter + 0.3 * half + 0.2 * (half * half)


def pivot_panel(p, base, a, xi):
    first = pl.multiple_of(p * W, W)
    rows = pl.ds(first, W)
    lanes = B - base
    s = a[rows, base:]
    xs = xi[rows, :]
    sub = lax.broadcasted_iota(jnp.int32, (W, 1), 0)
    lane = lax.broadcasted_iota(jnp.int32, (W, lanes), 1) + base
    columns = [
        jnp.sum(jnp.where(lane == first + j, s, 0.0), axis=1, keepdims=True) for j in range(W)
    ]
    pivots = jnp.ones((W, 1), jnp.float32)
    for j in range(W):
        pivot = columns[j][j : j + 1]
        factor = jnp.where(sub > j, columns[j] * (1.0 / pivot), 0.0)
        for k in range(j + 1, W):
            columns[k] = columns[k] - factor * columns[k][j : j + 1]
        s = s - factor * s[j : j + 1]
        xs = xs - factor * xs[j : j + 1]
        pivots = jnp.where(sub == j, pivot, pivots)
    scale = lax.rsqrt(pivots)
    xs = xs * scale
    later = jnp.where(lane >= first + W, s * scale, 0.0)
    update = product(
        split(later, 3), split(jnp.concatenate([later, xs], axis=1), 3), (0, 0), 3
    )
    a[base:, base:] = a[base:, base:] - update[:, :lanes]
    xi[base:, :] = xi[base:, :] - update[:, lanes:]
    xi[rows, :] = xs


def eliminate(first, last, a, xi):
    base = 0 if last * W <= B // 2 else B // 2

    def step(p, carry):
        pivot_panel(p, base, a, xi)
        return carry

    lax.fori_loop(first, last, step, 0)


def code_parts(codes):
    codes = codes.astype(jnp.int32)
    high = (codes + 128) >> 8
    return high.astype(jnp.float32), (codes - high * 256).astype(jnp.float32)


def whole_kernel(
    owner_hbm, position_hbm, weights_hbm, features_hbm, factor_hbm, columns_out, gram_out,
    owner, position, weights, features, factor, factor_hi, factor_lo, norms, table,
    sx, sh, rx, rh, tx, th, ax, ah, bx, bh, yx, yh, fx, fh,
    px, pa, pb, rt, m, a, xi, f, cl, a1, xl, a2, zl, a3, yl,
    load_sem, send_sem, recv_sem,
):
    x, z, c, y = (coord(axis) for axis in AXES)
    copies = Copies(send_sem, recv_sem)
    small = [
        pltpu.make_async_copy(source, target, load_sem.at[5 + i])
        for i, (source, target) in enumerate(
            ((owner_hbm, owner), (position_hbm, position), (weights_hbm, weights))
        )
    ]
    for load in small:
        load.start()
    load_x = pltpu.make_async_copy(features_hbm, features, load_sem.at[0])
    load_x.start()
    loads = []
    for i in range(4):
        rows = pl.ds(i * 128, 128)
        loads.append(
            pltpu.make_async_copy(factor_hbm.at[rows], factor.at[rows], load_sem.at[1 + i])
        )
        loads[i].start()
    wait_for_all = greet([peer(**o) for o in ZC_PEERS + X_PEERS + Y_PEERS])
    sibling = peer(**CORE)

    me = ((x * 8 + z) * 2 + c) * 8 + y
    for load in small:
        load.wait()
    row_owner = owner[...]
    col_owner = jnp.broadcast_to(row_owner.astype(jnp.float32), (B, B)).T.astype(jnp.int32)
    i_row = lax.broadcasted_iota(jnp.int32, (B, B), 0)
    i_col = lax.broadcasted_iota(jnp.int32, (B, B), 1)
    same = col_owner == row_owner
    row_rank = jnp.sum(jnp.where(same & (i_row < i_col), 1.0, 0.0), axis=0, keepdims=True)
    col_rank = jnp.sum(jnp.where(same & (i_col < i_row), 1.0, 0.0), axis=1, keepdims=True)
    near = (col_owner[:, :128] // 128 == x) & (col_owner[:, :128] % 8 == y)
    place = (col_owner[:, :128] // 8) % 16 * 4 + col_rank.astype(jnp.int32)
    table[...] = jnp.where(near, place, -64)

    slot = lax.broadcasted_iota(jnp.int32, (48, B), 0)
    slot = jnp.where(slot < 16, slot // 4, (slot - 16) // 8)
    mine = (row_owner == me) & (row_rank.astype(jnp.int32) == slot)
    at = jnp.sum(
        jnp.where(mine, position[...].astype(jnp.float32) + 1.0, 0.0), axis=1, keepdims=True
    ).astype(jnp.int32) - 1
    pick = jnp.where(lax.broadcasted_iota(jnp.int32, (48, 512), 1) == at, 1.0, 0.0).astype(jnp.bfloat16)
    load_x.wait()
    rows_x = jnp.dot(pick[:16], features[...], preferred_element_type=jnp.float32)
    block_x = lax.broadcasted_iota(jnp.int32, (16, 128), 0) % 4
    sx[...] = sum(
        jnp.where(block_x == b, rows_x[:, b * 128 : b * 128 + 128], 0.0) for b in range(4)
    ).astype(jnp.bfloat16)
    for load in loads:
        load.wait()

    def cut(i, carry):
        rows = pl.ds(pl.multiple_of(i * 64, 64), 64)
        factor_hi[rows, :], factor_lo[rows, :] = split(factor[rows, :], 2)
        return carry

    lax.fori_loop(0, 8, cut, 0)
    rows_h = jnp.dot(pick[16:], factor_hi[...], preferred_element_type=jnp.float32) + jnp.dot(
        pick[16:], factor_lo[...], preferred_element_type=jnp.float32
    )
    block_h = lax.broadcasted_iota(jnp.int32, (32, 128), 0) % 8
    own_h = sum(jnp.where(block_h == b, rows_h[:, b * 128 : b * 128 + 128], 0.0) for b in range(8))
    sh[...] = jnp.round(own_h * H_SCALE).astype(jnp.int32).astype(jnp.int16)

    wait_for_all()
    here = z * 2 + c
    pending = []
    for o in ZC_PEERS:
        pending.append(copies.start(sx, rx.at[here], peer(**o)))
        pending.append(copies.start(sh, rh.at[here], peer(**o)))
    rx[here] = sx[...]
    rh[here] = sh[...]
    norms[...] = row_norms(features[...])
    target = table[pl.ds(pl.multiple_of(here * 16, 16), 16), :][:, :1]
    target_x = jnp.concatenate([target * 4 + b for b in range(4)], axis=0)
    target_h = jnp.concatenate([target * 8 + b for b in range(8)], axis=0)
    pick_x = jnp.where(
        lax.broadcasted_iota(jnp.int32, (64, 256), 1) == target_x, 1.0, 0.0
    ).astype(jnp.bfloat16)
    pick_h = jnp.where(
        lax.broadcasted_iota(jnp.int32, (128, 512), 1) == target_h, 1.0, 0.0
    ).astype(jnp.bfloat16)
    for copy in pending:
        copy.wait()
    tx[...] = jnp.dot(
        pick_x, rx[...].reshape(16 * 16, 128), preferred_element_type=jnp.float32
    ).astype(jnp.bfloat16).reshape(4, 16, 128)
    high, low = code_parts(rh[...].reshape(16 * 32, 128))
    picked = 256.0 * jnp.dot(
        pick_h, high.astype(jnp.bfloat16), preferred_element_type=jnp.float32
    ) + jnp.dot(pick_h, low.astype(jnp.bfloat16), preferred_element_type=jnp.float32)
    th[...] = picked.astype(jnp.int32).astype(jnp.int16).reshape(4, 2, 16, 128)

    pending = []
    for i, o in enumerate(X_PEERS):
        device = peer(**o)
        pending.append(copies.start(tx.at[device[0]], ax.at[i], device))
        pending.append(copies.start(th.at[device[0]], ah.at[i], device))
    for copy in pending:
        copy.wait()
    total_x = tx[x].astype(jnp.float32)
    total_h = th[x].astype(jnp.int32)
    for i in range(3):
        total_x = total_x + ax[i].astype(jnp.float32)
        total_h = total_h + ah[i].astype(jnp.int32)
    bx[...] = total_x.astype(jnp.bfloat16)
    bh[...] = total_h.astype(jnp.int16)

    pending = []
    for i, o in enumerate(Y_PEERS):
        pending.append(copies.start(bx, yx.at[i], peer(**o)))
        pending.append(copies.start(bh, yh.at[i], peer(**o)))
    for copy in pending:
        copy.wait()
    for i in range(7):
        total_x = total_x + yx[i].astype(jnp.float32)
        total_h = total_h + yh[i].astype(jnp.int32)
    fx[c, x, 0] = total_x.astype(jnp.bfloat16)
    fh[c, x, 0] = total_h.astype(jnp.int16)

    along_z = []
    for i, o in enumerate(Z_PEERS):
        along_z.append(copies.start(fx.at[c, x, 0], fx.at[c, x, i + 1], peer(**o)))
        along_z.append(copies.start(fh.at[c, x, 0], fh.at[c, x, i + 1], peer(**o)))
    along_x, across = [], []
    for first, size in Z_GROUPS:
        for i in range(max(first, 1), first + size):
            along_z[2 * i - 2].wait_recv()
            along_z[2 * i - 1].wait_recv()
        part_x, part_h = (ref.at[c, x, pl.ds(first, size)] for ref in (fx, fh))
        for o in X_PEERS:
            along_x.append(copies.start(part_x, part_x, peer(**o)))
            along_x.append(copies.start(part_h, part_h, peer(**o)))
        across.append(copies.start(part_x, part_x, sibling))
        across.append(copies.start(part_h, part_h, sibling))
    for g, (first, size) in enumerate(Z_GROUPS):
        for i, o in enumerate(X_PEERS):
            source = lax.rem(x + 4 - o["x"], 4)
            for j, ref in enumerate((fx, fh)):
                part = ref.at[c, source, pl.ds(first, size)]
                along_x[(g * 3 + i) * 2 + j].wait_recv()
                across.append(copies.start(part, part, sibling))

    def unpack(core):
        def step(i, carry):
            odd = i % 2
            back = odd * ((i + 1) // 2) + (1 - odd) * (8 - i // 2)
            rows = pl.ds(pl.multiple_of((((z + 8 - back) % 8) * 2 + core) * 16, 16), 16)
            for xb in range(4):
                px[rows, xb * 128 : xb * 128 + 128] = fx[core, xb, i]
                for j in range(2):
                    high, low = code_parts(fh[core, xb, i, j])
                    at = (xb * 2 + j) * 128
                    pa[rows, at : at + 128] = (high * (256.0 / H_SCALE)).astype(jnp.bfloat16)
                    pb[rows, at : at + 128] = (low * (1.0 / H_SCALE)).astype(jnp.bfloat16)
            return carry

        lax.fori_loop(0, 8, step, 0)

    unpack(c)
    for copy in along_z + along_x:
        copy.wait_send()
    for copy in across:
        copy.wait()
    unpack(1 - c)

    def local(i, carry):
        span = pl.ds(pl.multiple_of(i * 256, 256), 256)
        h = [factor_hi[span, :], factor_lo[span, :]]
        residual = transposed_kernel(px[...], features[span, :], norms[:, span]) - product(
            [pa[...], pb[...]], h, (1, 1), 2
        )
        rt[i] = residual
        weighted = split(residual * weights[i], 2)
        left = product(weighted, h, (1, 0), 2)
        right = product(weighted, split(residual, 2), (1, 1), 2)
        both = jnp.concatenate([left, right], axis=1)
        for k in range(10):
            m[k] = m[k] + both[:, k * 128 : k * 128 + 128].reshape(4, 8, 8, 128)
        return carry

    m[...] = jnp.zeros_like(m)
    lax.fori_loop(0, 2, local, 0)

    def core_out(o, n):
        return [copies.start(m.at[pl.ds(5 * (1 - c) + o, n)], cl.at[pl.ds(o, n)], sibling)]

    def core_in(o, n):
        a1[o : o + n] = m[pl.ds(5 * c + o, n)] + cl[o : o + n]

    def x_out(o, n):
        return [
            copies.start(a1.at[pl.ds(o, n), peer(**p)[0]], xl.at[i, pl.ds(o, n)], peer(**p))
            for i, p in enumerate(X_PEERS)
        ]

    def x_in(o, n):
        a2[o : o + n] = a1[o : o + n, x] + xl[0, o : o + n] + xl[1, o : o + n] + xl[2, o : o + n]

    def z_out(o, n):
        return [
            copies.start(a2.at[pl.ds(o, n), peer(**p)[1]], zl.at[i, pl.ds(o, n)], peer(**p))
            for i, p in enumerate(Z_PEERS)
        ]

    def z_in(o, n):
        total = a2[o : o + n, z]
        for i in range(7):
            total = total + zl[i, o : o + n]
        a3[o : o + n] = total
        yl[y, o : o + n] = total

    def y_out(o, n):
        return [copies.start(a3.at[pl.ds(o, n)], yl.at[y, pl.ds(o, n)], peer(**p)) for p in Y_PEERS]

    def y_in(o, n):
        total = yl[0, o : o + n]
        for i in range(1, 8):
            total = total + yl[i, o : o + n]
        f[pl.ds(5 * c + o, n), x, z] = total

    def back(o, n, place, peers):
        block = f.at[(pl.ds(5 * c + o, n), *place)]
        return [copies.start(block, block, peer(**p)) for p in peers]

    def begin_block():
        h = [pa[...], pb[...]]
        a[...] = transposed_kernel(px[...], px[...], row_norms(px[...])) - product(h, h, (1, 1), 2)
        row = lax.broadcasted_iota(jnp.int32, (B, B), 0)
        column = lax.broadcasted_iota(jnp.int32, (B, B), 1)
        xi[...] = jnp.where(row == column, 1.0, 0.0)

    def columns_of(i):
        flipped = product(split(xi[...], 3), split(rt[i], 3), (1, 0), 3)
        columns_out[i * 256 : (i + 1) * 256, :] = flipped.T

    beside = [
        [begin_block, lambda: eliminate(0, 2, a, xi)],
        [lambda: eliminate(2, 8, a, xi)],
        [lambda: eliminate(8, 12, a, xi)],
        [lambda: eliminate(12, 16, a, xi)],
        [lambda: columns_of(0)],
        [lambda: columns_of(1)],
        [],
    ]
    stages = [
        (core_out, core_in),
        (x_out, x_in),
        (z_out, z_in),
        (y_out, y_in),
        (lambda o, n: back(o, n, (x, z), Z_PEERS), None),
        (lambda o, n: back(o, n, (x,), X_PEERS), None),
        (lambda o, n: back(o, n, (), [CORE]), None),
    ]
    flying = {chunk: stages[0][0](*chunk) for chunk in CHUNKS}
    for s in range(len(stages)):
        for work in beside[s]:
            work()
        for chunk in CHUNKS:
            for copy in flying[chunk]:
                copy.wait()
            if stages[s][1] is not None:
                stages[s][1](*chunk)
            if s + 1 < len(stages):
                flying[chunk] = stages[s + 1][0](*chunk)

    inverse = split(xi[...], 3)
    scaled = 1.0 / (512 * 512)

    def total_of(k):
        return jnp.concatenate([f[k].reshape(B, 128), f[k + 1].reshape(B, 128)], axis=1)

    for k in range(0, 8, 2):
        gram_out[:, k * 128 : k * 128 + 256] = scaled * product(inverse, split(total_of(k), 3), (1, 0), 3)
    right = product(inverse, split(total_of(8), 3), (1, 0), 3)
    gram_out[:, R:] = scaled * product(split(right, 3), inverse, (1, 1), 3)


def run(features, factor, ip_weights, pivot_owner, pivot_position):
    count = 92 + len(CHUNKS) * 29
    vmem = pl.BlockSpec(memory_space=pltpu.VMEM)
    hbm = pl.BlockSpec(memory_space=pltpu.HBM)
    f32, bf16, i16 = jnp.float32, jnp.bfloat16, jnp.int16
    return pl.pallas_call(
        whole_kernel,
        out_shape=(
            jax.ShapeDtypeStruct((512, B), f32),
            jax.ShapeDtypeStruct((B, R + B), f32),
        ),
        in_specs=[hbm] * 5,
        out_specs=(vmem, vmem),
        scratch_shapes=[
            pltpu.VMEM((1, B), jnp.int32),
            pltpu.VMEM((1, B), jnp.int32),
            pltpu.VMEM((2, 1, 256), f32),
            pltpu.VMEM((512, F), bf16),
            pltpu.VMEM((512, R), f32),
            pltpu.VMEM((512, R), bf16),
            pltpu.VMEM((512, R), bf16),
            pltpu.VMEM((1, 512), f32),
            pltpu.VMEM((B, 128), jnp.int32),
            pltpu.VMEM((16, 128), bf16),
            pltpu.VMEM((32, 128), i16),
            pltpu.VMEM((16, 16, 128), bf16),
            pltpu.VMEM((16, 32, 128), i16),
            pltpu.VMEM((4, 16, 128), bf16),
            pltpu.VMEM((4, 2, 16, 128), i16),
            pltpu.VMEM((3, 16, 128), bf16),
            pltpu.VMEM((3, 2, 16, 128), i16),
            pltpu.VMEM((16, 128), bf16),
            pltpu.VMEM((2, 16, 128), i16),
            pltpu.VMEM((7, 16, 128), bf16),
            pltpu.VMEM((7, 2, 16, 128), i16),
            pltpu.VMEM((2, 4, 8, 16, 128), bf16),
            pltpu.VMEM((2, 4, 8, 2, 16, 128), i16),
            pltpu.VMEM((B, F), bf16),
            pltpu.VMEM((B, R), bf16),
            pltpu.VMEM((B, R), bf16),
            pltpu.VMEM((2, B, 256), f32),
            pltpu.VMEM((10, 4, 8, 8, 128), f32),
            pltpu.VMEM((B, B), f32),
            pltpu.VMEM((B, B), f32),
            pltpu.VMEM((10, 4, 8, 8, 128), f32),
            pltpu.VMEM((5, 4, 8, 8, 128), f32),
            pltpu.VMEM((5, 4, 8, 8, 128), f32),
            pltpu.VMEM((3, 5, 8, 8, 128), f32),
            pltpu.VMEM((5, 8, 8, 128), f32),
            pltpu.VMEM((7, 5, 8, 128), f32),
            pltpu.VMEM((5, 8, 128), f32),
            pltpu.VMEM((8, 5, 8, 128), f32),
            pltpu.SemaphoreType.DMA((8,)),
            pltpu.SemaphoreType.DMA((count,)),
            pltpu.SemaphoreType.DMA((count,)),
        ],
        compiler_params=pltpu.CompilerParams(
            collective_id=0, has_side_effects=True, vmem_limit_bytes=56 * 2**20
        ),
    )(
        pivot_owner.reshape(1, B),
        pivot_position.reshape(1, B),
        ip_weights.reshape(2, 1, 256),
        features,
        factor,
    )


def solution(mesh):
    torus = Mesh(mesh.devices.reshape(4, 8, 2, 8), AXES)
    in_specs = (P(AXES, None), P(AXES, None), P(AXES), P(), P())
    out_specs = (P(AXES, None), P())
    return jax.shard_map(run, mesh=torus, in_specs=in_specs, out_specs=out_specs, check_vma=False)
```

```python
import jax
import jax.numpy as jnp
from jax import lax
from jax.experimental import pallas as pl
from jax.experimental.pallas import tpu as pltpu
from jax.sharding import Mesh
from jax.sharding import PartitionSpec as P

MESH = pl.DeviceIdType.MESH
AXES = ("x", "z", "c", "y")
SIZES = {"x": 4, "z": 8, "c": 2, "y": 8}
F = 512
R = 1024
B = 256
H_SCALE = 2.0**20


def coord(axis):
    return lax.axis_index(axis)


def peer(**offsets):
    return tuple(
        lax.rem(coord(a) + offsets[a] % SIZES[a], SIZES[a]) if a in offsets else coord(a) for a in AXES
    )


class Copies:
    def __init__(self, send_sem, recv_sem):
        self.send_sem, self.recv_sem, self.used = send_sem, recv_sem, 0

    def start(self, src, dst, device):
        copy = pltpu.make_async_remote_copy(
            src_ref=src,
            dst_ref=dst,
            send_sem=self.send_sem.at[self.used],
            recv_sem=self.recv_sem.at[self.used],
            device_id=device,
            device_id_type=MESH,
        )
        self.used += 1
        copy.start()
        return copy


def greet(peers):
    barrier = pltpu.get_barrier_semaphore()
    for device in peers:
        pl.semaphore_signal(barrier, inc=1, device_id=device, device_id_type=MESH)
    return lambda: pl.semaphore_wait(barrier, len(peers))


X_PEERS = [dict(x=d) for d in (1, 3, 2)]
Y_PEERS = [dict(y=d) for d in range(1, 8)]
Z_STEPS = (0, 1, 7, 2, 6, 3, 5, 4)
Z_PEERS = [dict(z=d) for d in Z_STEPS[1:]]
XC_PEERS = [dict(x=d, c=e) for d in (0, 1, 3, 2) for e in range(2) if (d, e) != (0, 0)]
CORE = dict(c=1)
Z_GROUPS = ((0, 5), (5, 3))


W = 16


def split(values, count):
    out = []
    for _ in range(count - 1):
        part = values.astype(jnp.bfloat16)
        out.append(part)
        values = values - part.astype(jnp.float32)
    return out + [values.astype(jnp.bfloat16)]


def product(left, right, dims, count):
    order = {2: ((0, 0), (0, 1), (1, 0)), 3: ((0, 0), (0, 1), (1, 0), (0, 2), (2, 0), (1, 1))}[count]
    lhs = jnp.concatenate([left[i] for i, _ in order], axis=dims[0])
    rhs = jnp.concatenate([right[j] for _, j in order], axis=dims[1])
    return lax.dot_general(
        lhs, rhs, (((dims[0],), (dims[1],)), ((), ())), preferred_element_type=jnp.float32
    )


def row_norms(samples):
    ones = jnp.ones((8, F), jnp.bfloat16)
    norms = sum(
        lax.dot_general(ones, s, (((1,), (1,)), ((), ())), preferred_element_type=jnp.float32)
        for s in split(jnp.square(samples.astype(jnp.float32)), 2)
    )
    return norms[0:1]


def transposed_kernel(pivots, samples, norms):
    cross = lax.dot_general(
        pivots, samples, (((1,), (1,)), ((), ())), preferred_element_type=jnp.float32
    )
    pivot_norms = jnp.sum(jnp.square(pivots.astype(jnp.float32)), axis=1, keepdims=True)
    distance = pivot_norms + norms - 2.0 * cross
    quarter = jnp.exp(-(0.25 / F) * distance)
    half = quarter * quarter
    return 0.5 * quarter + 0.3 * half + 0.2 * (half * half)


def pivot_panel(p, base, a, xi):
    first = pl.multiple_of(p * W, W)
    rows = pl.ds(first, W)
    lanes = B - base
    s = a[rows, base:]
    xs = xi[rows, :]
    sub = lax.broadcasted_iota(jnp.int32, (W, 1), 0)
    lane = lax.broadcasted_iota(jnp.int32, (W, lanes), 1) + base
    columns = [
        jnp.sum(jnp.where(lane == first + j, s, 0.0), axis=1, keepdims=True) for j in range(W)
    ]
    pivots = jnp.ones((W, 1), jnp.float32)
    for j in range(W):
        pivot = columns[j][j : j + 1]
        factor = jnp.where(sub > j, columns[j] * (1.0 / pivot), 0.0)
        for k in range(j + 1, W):
            columns[k] = columns[k] - factor * columns[k][j : j + 1]
        s = s - factor * s[j : j + 1]
        xs = xs - factor * xs[j : j + 1]
        pivots = jnp.where(sub == j, pivot, pivots)
    scale = lax.rsqrt(pivots)
    xs = xs * scale
    later = jnp.where(lane >= first + W, s * scale, 0.0)
    update = product(
        split(later, 3), split(jnp.concatenate([later, xs], axis=1), 3), (0, 0), 3
    )
    a[base:, base:] = a[base:, base:] - update[:, :lanes]
    xi[base:, :] = xi[base:, :] - update[:, lanes:]
    xi[rows, :] = xs


def eliminate(first, last, a, xi):
    base = 0 if last * W <= B // 2 else B // 2

    def step(p, carry):
        pivot_panel(p, base, a, xi)
        return carry

    lax.fori_loop(first, last, step, 0)


def code_parts(codes):
    codes = codes.astype(jnp.int32)
    high = (codes + 128) >> 8
    return high.astype(jnp.float32), (codes - high * 256).astype(jnp.float32)


def whole_kernel(
    owner_hbm, position_hbm, weights_hbm, features_hbm, factor_hbm, columns_out, gram_out,
    owner, position, weights, features, factor, factor_hi, factor_lo, norms, table,
    sx, sh, rx, rh, tx, th, ax, ah, bx, bh, yx, yh, fx, fh,
    px, pa, pb, rt, m, a, xi, f, cl, a1,
    lx1, sx1, lx2, sx2, lx3, mx1, nx1, mx2, nx2, mx3, lz1, sz1, lz2, sz2, lz3, ly1, sy1, ly2, sy2, ly3,
    load_sem, send_sem, recv_sem,
):
    x, z, c, y = (coord(axis) for axis in AXES)
    copies = Copies(send_sem, recv_sem)
    small = [
        pltpu.make_async_copy(source, target, load_sem.at[5 + i])
        for i, (source, target) in enumerate(
            ((owner_hbm, owner), (position_hbm, position), (weights_hbm, weights))
        )
    ]
    for load in small:
        load.start()
    load_x = pltpu.make_async_copy(features_hbm, features, load_sem.at[0])
    load_x.start()
    loads = []
    for i in range(4):
        rows = pl.ds(i * 128, 128)
        loads.append(
            pltpu.make_async_copy(factor_hbm.at[rows], factor.at[rows], load_sem.at[1 + i])
        )
        loads[i].start()
    wait_for_all = greet([peer(**o) for o in XC_PEERS + Y_PEERS + Z_PEERS])
    sibling = peer(**CORE)

    me = ((x * 8 + z) * 2 + c) * 8 + y
    for load in small:
        load.wait()
    row_owner = owner[...]
    col_owner = jnp.broadcast_to(row_owner.astype(jnp.float32), (B, B)).T.astype(jnp.int32)
    i_row = lax.broadcasted_iota(jnp.int32, (B, B), 0)
    i_col = lax.broadcasted_iota(jnp.int32, (B, B), 1)
    same = col_owner == row_owner
    row_rank = jnp.sum(jnp.where(same & (i_row < i_col), 1.0, 0.0), axis=0, keepdims=True)
    col_rank = jnp.sum(jnp.where(same & (i_col < i_row), 1.0, 0.0), axis=1, keepdims=True)
    near = col_owner[:, :128] // 128 == x
    near = near & (col_owner[:, :128] % 8 == y) & ((col_owner[:, :128] // 8) % 2 == c)
    place = (col_owner[:, :128] // 16) % 8 * 4 + col_rank.astype(jnp.int32)
    table[...] = jnp.where(near, place, -64)

    slot = lax.broadcasted_iota(jnp.int32, (48, B), 0)
    slot = jnp.where(slot < 16, slot // 4, (slot - 16) // 8)
    mine = (row_owner == me) & (row_rank.astype(jnp.int32) == slot)
    at = jnp.sum(
        jnp.where(mine, position[...].astype(jnp.float32) + 1.0, 0.0), axis=1, keepdims=True
    ).astype(jnp.int32) - 1
    pick = jnp.where(lax.broadcasted_iota(jnp.int32, (48, 512), 1) == at, 1.0, 0.0).astype(jnp.bfloat16)
    load_x.wait()
    rows_x = jnp.dot(pick[:16], features[...], preferred_element_type=jnp.float32)
    block_x = lax.broadcasted_iota(jnp.int32, (16, 128), 0) % 4
    sx[...] = sum(
        jnp.where(block_x == b, rows_x[:, b * 128 : b * 128 + 128], 0.0) for b in range(4)
    ).astype(jnp.bfloat16)
    for load in loads:
        load.wait()

    def cut(i, carry):
        rows = pl.ds(pl.multiple_of(i * 64, 64), 64)
        factor_hi[rows, :], factor_lo[rows, :] = split(factor[rows, :], 2)
        return carry

    lax.fori_loop(0, 8, cut, 0)
    rows_h = jnp.dot(pick[16:], factor_hi[...], preferred_element_type=jnp.float32) + jnp.dot(
        pick[16:], factor_lo[...], preferred_element_type=jnp.float32
    )
    block_h = lax.broadcasted_iota(jnp.int32, (32, 128), 0) % 8
    own_h = sum(jnp.where(block_h == b, rows_h[:, b * 128 : b * 128 + 128], 0.0) for b in range(8))
    sh[...] = jnp.round(own_h * H_SCALE).astype(jnp.int32).astype(jnp.int16)

    wait_for_all()
    pending = []
    for o in Z_PEERS:
        pending.append(copies.start(sx, rx.at[z], peer(**o)))
        pending.append(copies.start(sh, rh.at[z], peer(**o)))
    rx[z] = sx[...]
    rh[z] = sh[...]
    norms[...] = row_norms(features[...])
    target = table[pl.ds(pl.multiple_of(z * 32, 32), 32), :][:, :1]
    halves = [target[:16], target[16:]]
    target_x = jnp.concatenate([target * 4 + b for b in range(4)], axis=0)
    target_h = jnp.concatenate(
        [half * 8 + (2 * b + j) for b in range(4) for half in halves for j in range(2)], axis=0
    )
    pick_x = jnp.where(
        lax.broadcasted_iota(jnp.int32, (128, 128), 1) == target_x, 1.0, 0.0
    ).astype(jnp.bfloat16)
    pick_h = jnp.where(
        lax.broadcasted_iota(jnp.int32, (256, 256), 1) == target_h, 1.0, 0.0
    ).astype(jnp.bfloat16)
    for copy in pending:
        copy.wait()
    tx[...] = jnp.dot(
        pick_x, rx[...].reshape(8 * 16, 128), preferred_element_type=jnp.float32
    ).astype(jnp.bfloat16).reshape(4, 2, 16, 128)
    high, low = code_parts(rh[...].reshape(8 * 32, 128))
    picked = 256.0 * jnp.dot(
        pick_h, high.astype(jnp.bfloat16), preferred_element_type=jnp.float32
    ) + jnp.dot(pick_h, low.astype(jnp.bfloat16), preferred_element_type=jnp.float32)
    th[...] = picked.astype(jnp.int32).astype(jnp.int16).reshape(4, 2, 2, 16, 128)

    pending = []
    for i, o in enumerate(XC_PEERS):
        device = peer(**o)
        pending.append(copies.start(tx.at[device[0], device[2]], ax.at[i], device))
        pending.append(copies.start(th.at[device[0], device[2]], ah.at[i], device))
    for copy in pending:
        copy.wait()
    total_x = tx[x, c].astype(jnp.float32)
    total_h = th[x, c].astype(jnp.int32)
    for i in range(7):
        total_x = total_x + ax[i].astype(jnp.float32)
        total_h = total_h + ah[i].astype(jnp.int32)
    bx[...] = total_x.astype(jnp.bfloat16)
    bh[...] = total_h.astype(jnp.int16)

    pending = []
    for i, o in enumerate(Y_PEERS):
        pending.append(copies.start(bx, yx.at[i], peer(**o)))
        pending.append(copies.start(bh, yh.at[i], peer(**o)))
    for copy in pending:
        copy.wait()
    for i in range(7):
        total_x = total_x + yx[i].astype(jnp.float32)
        total_h = total_h + yh[i].astype(jnp.int32)
    fx[c, 0, x] = total_x.astype(jnp.bfloat16)
    fh[c, x, 0] = total_h.astype(jnp.int16)

    x_first = [copies.start(fx.at[c, 0, x], fx.at[c, 0, x], peer(**o)) for o in X_PEERS]
    z_first = [copies.start(fh.at[c, x, 0], fh.at[c, x, i + 1], peer(**o)) for i, o in enumerate(Z_PEERS)]
    for copy in x_first:
        copy.wait_recv()
    z_second = [copies.start(fx.at[c, 0], fx.at[c, i + 1], peer(**o)) for i, o in enumerate(Z_PEERS)]
    x_second, across = [], []
    for first, size in Z_GROUPS:
        for i in range(max(first, 1), first + size):
            z_first[i - 1].wait_recv()
        part = fh.at[c, x, pl.ds(first, size)]
        for o in X_PEERS:
            x_second.append(copies.start(part, part, peer(**o)))
        across.append(copies.start(part, part, sibling))
    for first, size in Z_GROUPS:
        for i in range(max(first, 1), first + size):
            z_second[i - 1].wait_recv()
        part = fx.at[c, pl.ds(first, size)]
        across.append(copies.start(part, part, sibling))
    for g, (first, size) in enumerate(Z_GROUPS):
        for i, o in enumerate(X_PEERS):
            source = lax.rem(x + 4 - o["x"], 4)
            part = fh.at[c, source, pl.ds(first, size)]
            x_second[g * 3 + i].wait_recv()
            across.append(copies.start(part, part, sibling))

    def unpack(core):
        def step(i, carry):
            odd = i % 2
            back = odd * ((i + 1) // 2) + (1 - odd) * (8 - i // 2)
            rows = pl.ds(pl.multiple_of((((z + 8 - back) % 8) * 2 + core) * 16, 16), 16)
            for xb in range(4):
                px[rows, xb * 128 : xb * 128 + 128] = fx[core, i, xb]
                for j in range(2):
                    high, low = code_parts(fh[core, xb, i, j])
                    at = (xb * 2 + j) * 128
                    pa[rows, at : at + 128] = (high * (256.0 / H_SCALE)).astype(jnp.bfloat16)
                    pb[rows, at : at + 128] = (low * (1.0 / H_SCALE)).astype(jnp.bfloat16)
            return carry

        lax.fori_loop(0, 8, step, 0)

    unpack(c)
    for copy in x_first + z_first + z_second + x_second:
        copy.wait_send()
    for copy in across:
        copy.wait()
    unpack(1 - c)

    def local(i, carry):
        span = pl.ds(pl.multiple_of(i * 256, 256), 256)
        h = [factor_hi[span, :], factor_lo[span, :]]
        residual = transposed_kernel(px[...], features[span, :], norms[:, span]) - product(
            [pa[...], pb[...]], h, (1, 1), 2
        )
        rt[i] = residual
        weighted = split(residual * weights[i], 2)
        left = product(weighted, h, (1, 0), 2)
        right = product(weighted, split(residual, 2), (1, 1), 2)
        both = jnp.concatenate([left, right], axis=1)
        for k in range(10):
            m[k] = m[k] + both[:, k * 128 : k * 128 + 128].reshape(4, 8, 8, 128)
        return carry

    m[...] = jnp.zeros_like(m)
    lax.fori_loop(0, 2, local, 0)

    axis_at = dict(x=x, y=y, z=z)
    axis_peers = dict(x=X_PEERS, y=Y_PEERS, z=Z_PEERS)

    class Chunk:
        def __init__(self, o, n, first, second, last, land1, sum1, land2, sum2, land3):
            self.o, self.n = o, n
            self.first, self.second, self.last = first, second, last
            self.land1, self.sum1, self.land2, self.sum2, self.land3 = land1, sum1, land2, sum2, land3
            self.wide = second if first == "x" else first
            self.flying = []

        def line(self, ref, start, along, index):
            block = (pl.ds(start, self.n),)
            return ref.at[block + ((index,) if along == "x" else (slice(None), index))]

        def go(self, pairs):
            self.flying = [copies.start(source, target, device) for source, target, device in pairs]

        def land(self):
            for copy in self.flying:
                copy.wait()

        def targets(self, axis):
            where = AXES.index(axis)
            return [(i, peer(**o)[where], peer(**o)) for i, o in enumerate(axis_peers[axis])]

        def core_out(self):
            theirs = m.at[pl.ds(5 * (1 - c) + self.o, self.n)]
            self.go([(theirs, cl.at[pl.ds(self.o, self.n)], sibling)])

        def first_out(self):
            self.land()
            span = pl.ds(self.o, self.n)
            a1[span] = m[pl.ds(5 * c + self.o, self.n)] + cl[span]
            self.go([
                (self.line(a1, self.o, self.first, at), self.land1.at[i], device)
                for i, at, device in self.targets(self.first)
            ])

        def second_out(self):
            self.land()
            total = self.line(a1, self.o, self.first, axis_at[self.first])[...]
            for i in range(len(axis_peers[self.first])):
                total = total + self.land1[i]
            self.sum1[...] = total
            self.go([
                (self.sum1.at[:, at], self.land2.at[i], device)
                for i, at, device in self.targets(self.second)
            ])

        def last_out(self):
            self.land()
            total = self.sum1[:, axis_at[self.second]]
            for i in range(len(axis_peers[self.second])):
                total = total + self.land2[i]
            self.sum2[...] = total
            here = self.land3.at[axis_at[self.last]]
            here[...] = total
            self.go([(self.sum2, here, device) for _, _, device in self.targets(self.last)])

        def second_back(self):
            self.land()
            total = self.land3[0]
            for i in range(1, 8):
                total = total + self.land3[i]
            block = f.at[pl.ds(5 * c + self.o, self.n), x, axis_at[self.wide]]
            block[...] = total
            self.go([(block, block, device) for _, _, device in self.targets(self.second)])

        def first_back(self):
            self.land()
            block = self.line(f, 5 * c + self.o, self.first, axis_at[self.first])
            self.go([(block, block, device) for _, _, device in self.targets(self.first)])

        def core_back(self):
            if self.first != "x":
                self.land()
                block = f.at[pl.ds(5 * c + self.o, self.n)]
                self.go([(block, block, sibling)])
                return
            sent = self.flying
            block = self.line(f, 5 * c + self.o, "x", x)
            pairs = [copies.start(block, block, sibling)]
            for copy, o in zip(sent, X_PEERS):
                copy.wait_recv()
                block = self.line(f, 5 * c + self.o, "x", lax.rem(x + 4 - o["x"], 4))
                pairs.append(copies.start(block, block, sibling))
            for copy in sent:
                copy.wait_send()
            self.flying = pairs

    cx1 = Chunk(0, 2, "x", "z", "y", lx1, sx1, lx2, sx2, lx3)
    cx2 = Chunk(2, 1, "x", "z", "y", mx1, nx1, mx2, nx2, mx3)
    cz = Chunk(3, 1, "z", "x", "y", lz1, sz1, lz2, sz2, lz3)
    cy = Chunk(4, 1, "y", "x", "z", ly1, sy1, ly2, sy2, ly3)

    def begin_block():
        h = [pa[...], pb[...]]
        a[...] = transposed_kernel(px[...], px[...], row_norms(px[...])) - product(h, h, (1, 1), 2)
        row = lax.broadcasted_iota(jnp.int32, (B, B), 0)
        column = lax.broadcasted_iota(jnp.int32, (B, B), 1)
        xi[...] = jnp.where(row == column, 1.0, 0.0)

    def columns_of(i):
        flipped = product(split(xi[...], 3), split(rt[i], 3), (1, 0), 3)
        columns_out[i * 256 : (i + 1) * 256, :] = flipped.T

    for chunk in (cz, cy, cx1, cx2):
        chunk.core_out()
    for chunk in (cz, cy, cx1, cx2):
        chunk.first_out()
    begin_block()
    eliminate(0, 5, a, xi)
    for chunk in (cx1, cz, cy, cx2):
        chunk.second_out()
    eliminate(5, 8, a, xi)
    for chunk in (cz, cy, cx1, cx2):
        chunk.last_out()
    eliminate(8, 16, a, xi)
    for chunk in (cz, cy, cx1, cx2):
        chunk.second_back()
    columns_of(0)
    for chunk in (cz, cy, cx1, cx2):
        chunk.first_back()
    columns_of(1)
    for chunk in (cz, cy, cx1, cx2):
        chunk.core_back()

    inverse = split(xi[...], 3)
    scaled = 1.0 / (512 * 512)

    def applied(*blocks):
        total = jnp.concatenate([f[k].reshape(B, 128) for k in blocks], axis=1)
        return product(inverse, split(total, 3), (1, 0), 3)

    cz.land()
    cy.land()
    gram_out[:, 3 * 128 : 5 * 128] = scaled * applied(3, 4)
    gram_out[:, R:] = scaled * product(split(applied(8, 9), 3), inverse, (1, 1), 3)
    cx1.land()
    gram_out[:, :256] = scaled * applied(0, 1)
    gram_out[:, 5 * 128 : 7 * 128] = scaled * applied(5, 6)
    cx2.land()
    last = scaled * applied(2, 7)
    gram_out[:, 2 * 128 : 3 * 128] = last[:, :128]
    gram_out[:, 7 * 128 : 8 * 128] = last[:, 128:]


def sum_buffers(n, first, second):
    shapes = [
        (first, n, second, 8, 128),
        (n, second, 8, 128),
        (second - 1, n, 8, 128),
        (n, 8, 128),
        (8, n, 8, 128),
    ]
    return [pltpu.VMEM(shape, jnp.float32) for shape in shapes]


def run(features, factor, ip_weights, pivot_owner, pivot_position):
    count = 64 + 16 + 4 * 32
    vmem = pl.BlockSpec(memory_space=pltpu.VMEM)
    hbm = pl.BlockSpec(memory_space=pltpu.HBM)
    f32, bf16, i16 = jnp.float32, jnp.bfloat16, jnp.int16
    return pl.pallas_call(
        whole_kernel,
        out_shape=(
            jax.ShapeDtypeStruct((512, B), f32),
            jax.ShapeDtypeStruct((B, R + B), f32),
        ),
        in_specs=[hbm] * 5,
        out_specs=(vmem, vmem),
        scratch_shapes=[
            pltpu.VMEM((1, B), jnp.int32),
            pltpu.VMEM((1, B), jnp.int32),
            pltpu.VMEM((2, 1, 256), f32),
            pltpu.VMEM((512, F), bf16),
            pltpu.VMEM((512, R), f32),
            pltpu.VMEM((512, R), bf16),
            pltpu.VMEM((512, R), bf16),
            pltpu.VMEM((1, 512), f32),
            pltpu.VMEM((B, 128), jnp.int32),
            pltpu.VMEM((16, 128), bf16),
            pltpu.VMEM((32, 128), i16),
            pltpu.VMEM((8, 16, 128), bf16),
            pltpu.VMEM((8, 32, 128), i16),
            pltpu.VMEM((4, 2, 16, 128), bf16),
            pltpu.VMEM((4, 2, 2, 16, 128), i16),
            pltpu.VMEM((7, 16, 128), bf16),
            pltpu.VMEM((7, 2, 16, 128), i16),
            pltpu.VMEM((16, 128), bf16),
            pltpu.VMEM((2, 16, 128), i16),
            pltpu.VMEM((7, 16, 128), bf16),
            pltpu.VMEM((7, 2, 16, 128), i16),
            pltpu.VMEM((2, 8, 4, 16, 128), bf16),
            pltpu.VMEM((2, 4, 8, 2, 16, 128), i16),
            pltpu.VMEM((B, F), bf16),
            pltpu.VMEM((B, R), bf16),
            pltpu.VMEM((B, R), bf16),
            pltpu.VMEM((2, B, 256), f32),
            pltpu.VMEM((10, 4, 8, 8, 128), f32),
            pltpu.VMEM((B, B), f32),
            pltpu.VMEM((B, B), f32),
            pltpu.VMEM((10, 4, 8, 8, 128), f32),
            pltpu.VMEM((5, 4, 8, 8, 128), f32),
            pltpu.VMEM((5, 4, 8, 8, 128), f32),
            *sum_buffers(2, 3, 8),
            *sum_buffers(1, 3, 8),
            *sum_buffers(1, 7, 4),
            *sum_buffers(1, 7, 4),
            pltpu.SemaphoreType.DMA((8,)),
            pltpu.SemaphoreType.DMA((count,)),
            pltpu.SemaphoreType.DMA((count,)),
        ],
        compiler_params=pltpu.CompilerParams(
            collective_id=0, has_side_effects=True, vmem_limit_bytes=56 * 2**20
        ),
    )(
        pivot_owner.reshape(1, B),
        pivot_position.reshape(1, B),
        ip_weights.reshape(2, 1, 256),
        features,
        factor,
    )


def solution(mesh):
    torus = Mesh(mesh.devices.reshape(4, 8, 2, 8), AXES)
    in_specs = (P(AXES, None), P(AXES, None), P(AXES), P(), P())
    out_specs = (P(AXES, None), P())
    return jax.shard_map(run, mesh=torus, in_specs=in_specs, out_specs=out_specs, check_vma=False)
```

```python
import jax
import jax.numpy as jnp
from jax import lax
from jax.experimental import pallas as pl
from jax.experimental.pallas import tpu as pltpu
from jax.sharding import Mesh
from jax.sharding import PartitionSpec as P

MESH = pl.DeviceIdType.MESH
AXES = ("x", "z", "c", "y")
SIZES = {"x": 4, "z": 8, "c": 2, "y": 8}
F = 512
R = 1024
B = 256
H_SCALE = 2.0**20


def coord(axis):
    return lax.axis_index(axis)


def peer(**offsets):
    return tuple(
        lax.rem(coord(a) + offsets[a] % SIZES[a], SIZES[a]) if a in offsets else coord(a) for a in AXES
    )


class Copies:
    def __init__(self, send_sem, recv_sem):
        self.send_sem, self.recv_sem, self.used = send_sem, recv_sem, 0

    def start(self, src, dst, device):
        copy = pltpu.make_async_remote_copy(
            src_ref=src,
            dst_ref=dst,
            send_sem=self.send_sem.at[self.used],
            recv_sem=self.recv_sem.at[self.used],
            device_id=device,
            device_id_type=MESH,
        )
        self.used += 1
        copy.start()
        return copy


def greet(peers):
    barrier = pltpu.get_barrier_semaphore()
    for device in peers:
        pl.semaphore_signal(barrier, inc=1, device_id=device, device_id_type=MESH)
    return lambda: pl.semaphore_wait(barrier, len(peers))


X_PEERS = [dict(x=d) for d in (2, 1, 3)]
Y_PEERS = [dict(y=d) for d in (4, 3, 5, 2, 6, 1, 7)]
Z_PEERS = [dict(z=d) for d in (4, 3, 5, 2, 6, 1, 7)]
XC_PEERS = [dict(x=d, c=e) for d in (2, 1, 3, 0) for e in (1, 0) if (d, e) != (0, 0)]
Z_ORDER = [dict(z=d) for d in (1, 7, 2, 6, 3, 5, 4)]
CORE = dict(c=1)
Z_GROUPS = ((0, 5), (5, 3))


W = 16


def split(values, count):
    out = []
    for _ in range(count - 1):
        part = values.astype(jnp.bfloat16)
        out.append(part)
        values = values - part.astype(jnp.float32)
    return out + [values.astype(jnp.bfloat16)]


def product(left, right, dims, count):
    order = {2: ((0, 0), (0, 1), (1, 0)), 3: ((0, 0), (0, 1), (1, 0), (0, 2), (2, 0), (1, 1))}[count]
    lhs = jnp.concatenate([left[i] for i, _ in order], axis=dims[0])
    rhs = jnp.concatenate([right[j] for _, j in order], axis=dims[1])
    return lax.dot_general(
        lhs, rhs, (((dims[0],), (dims[1],)), ((), ())), preferred_element_type=jnp.float32
    )


def row_norms(samples):
    ones = jnp.ones((8, F), jnp.bfloat16)
    norms = sum(
        lax.dot_general(ones, s, (((1,), (1,)), ((), ())), preferred_element_type=jnp.float32)
        for s in split(jnp.square(samples.astype(jnp.float32)), 2)
    )
    return norms[0:1]


def transposed_kernel(pivots, samples, norms):
    cross = lax.dot_general(
        pivots, samples, (((1,), (1,)), ((), ())), preferred_element_type=jnp.float32
    )
    pivot_norms = jnp.sum(jnp.square(pivots.astype(jnp.float32)), axis=1, keepdims=True)
    distance = pivot_norms + norms - 2.0 * cross
    quarter = jnp.exp(-(0.25 / F) * distance)
    half = quarter * quarter
    return 0.5 * quarter + 0.3 * half + 0.2 * (half * half)


def pivot_panel(p, base, a, xi):
    first = pl.multiple_of(p * W, W)
    rows = pl.ds(first, W)
    lanes = B - base
    s = a[rows, base:]
    xs = xi[rows, :]
    sub = lax.broadcasted_iota(jnp.int32, (W, 1), 0)
    lane = lax.broadcasted_iota(jnp.int32, (W, lanes), 1) + base
    columns = [
        jnp.sum(jnp.where(lane == first + j, s, 0.0), axis=1, keepdims=True) for j in range(W)
    ]
    pivots = jnp.ones((W, 1), jnp.float32)
    for j in range(W):
        pivot = columns[j][j : j + 1]
        factor = jnp.where(sub > j, columns[j] * (1.0 / pivot), 0.0)
        for k in range(j + 1, W):
            columns[k] = columns[k] - factor * columns[k][j : j + 1]
        s = s - factor * s[j : j + 1]
        xs = xs - factor * xs[j : j + 1]
        pivots = jnp.where(sub == j, pivot, pivots)
    scale = lax.rsqrt(pivots)
    xs = xs * scale
    later = jnp.where(lane >= first + W, s * scale, 0.0)
    update = product(
        split(later, 3), split(jnp.concatenate([later, xs], axis=1), 3), (0, 0), 3
    )
    a[base:, base:] = a[base:, base:] - update[:, :lanes]
    xi[base:, :] = xi[base:, :] - update[:, lanes:]
    xi[rows, :] = xs


def eliminate(first, last, a, xi):
    base = 0 if last * W <= B // 2 else B // 2

    def step(p, carry):
        pivot_panel(p, base, a, xi)
        return carry

    lax.fori_loop(first, last, step, 0)


def code_parts(codes):
    codes = codes.astype(jnp.int32)
    high = (codes + 128) >> 8
    return high.astype(jnp.float32), (codes - high * 256).astype(jnp.float32)


def whole_kernel(
    owner_hbm, position_hbm, weights_hbm, features_hbm, factor_hbm, columns_out, gram_out,
    owner, position, weights, features, factor, factor_hi, factor_lo, norms, table,
    sx, sh, rx, rh, tx, th, ax, ah, bx, bh, yx, yh, fx, fh,
    px, pa, pb, rt, m, a, xi, f, cl, a1,
    lx1, sx1, lx2, sx2, lx3, mx1, nx1, mx2, nx2, mx3, lz1, sz1, lz2, sz2, lz3, ly1, sy1, ly2, sy2, ly3,
    load_sem, send_sem, recv_sem,
):
    x, z, c, y = (coord(axis) for axis in AXES)
    copies = Copies(send_sem, recv_sem)
    small = [
        pltpu.make_async_copy(source, target, load_sem.at[5 + i])
        for i, (source, target) in enumerate(
            ((owner_hbm, owner), (position_hbm, position), (weights_hbm, weights))
        )
    ]
    for load in small:
        load.start()
    load_x = pltpu.make_async_copy(features_hbm, features, load_sem.at[0])
    load_x.start()
    loads = []
    for i in range(4):
        rows = pl.ds(i * 128, 128)
        loads.append(
            pltpu.make_async_copy(factor_hbm.at[rows], factor.at[rows], load_sem.at[1 + i])
        )
        loads[i].start()
    wait_for_all = greet([peer(**o) for o in XC_PEERS + Y_PEERS + Z_PEERS])
    sibling = peer(**CORE)

    me = ((x * 8 + z) * 2 + c) * 8 + y
    for load in small:
        load.wait()
    row_owner = owner[...]
    col_owner = jnp.broadcast_to(row_owner.astype(jnp.float32), (B, B)).T.astype(jnp.int32)
    i_row = lax.broadcasted_iota(jnp.int32, (B, B), 0)
    i_col = lax.broadcasted_iota(jnp.int32, (B, B), 1)
    same = col_owner == row_owner
    row_rank = jnp.sum(jnp.where(same & (i_row < i_col), 1.0, 0.0), axis=0, keepdims=True)
    col_rank = jnp.sum(jnp.where(same & (i_col < i_row), 1.0, 0.0), axis=1, keepdims=True)
    near = col_owner[:, :128] // 128 == x
    near = near & (col_owner[:, :128] % 8 == y) & ((col_owner[:, :128] // 8) % 2 == c)
    place = (col_owner[:, :128] // 16) % 8 * 4 + col_rank.astype(jnp.int32)
    table[...] = jnp.where(near, place, -64)

    order = row_rank.astype(jnp.int32)
    spots = [
        jnp.sum(jnp.where((row_owner == me) & (order == s), position[...], 0)) for s in range(4)
    ]
    slot = lax.broadcasted_iota(jnp.int32, (16, 512), 0) // 4
    lane = lax.broadcasted_iota(jnp.int32, (16, 512), 1)
    wanted = jnp.where(slot == 0, spots[0], jnp.where(slot == 1, spots[1], jnp.where(slot == 2, spots[2], spots[3])))
    pick = jnp.where(lane == wanted, 1.0, 0.0).astype(jnp.bfloat16)
    load_x.wait()
    rows_x = jnp.dot(pick, features[...], preferred_element_type=jnp.float32)
    block_x = lax.broadcasted_iota(jnp.int32, (16, 128), 0) % 4
    sx[...] = sum(
        jnp.where(block_x == b, rows_x[:, b * 128 : b * 128 + 128], 0.0) for b in range(4)
    ).astype(jnp.bfloat16)
    for load in loads:
        load.wait()
    rows_h = [factor[pl.ds(spot, 1), :] for spot in spots]
    own_h = jnp.concatenate(
        [row[:, b * 128 : b * 128 + 128] for row in rows_h for b in range(8)], axis=0
    )
    sh[...] = jnp.round(own_h * H_SCALE).astype(jnp.int32).astype(jnp.int16)

    wait_for_all()
    pending = []
    for o in Z_PEERS:
        pending.append(copies.start(sx, rx.at[z], peer(**o)))
        pending.append(copies.start(sh, rh.at[z], peer(**o)))
    rx[z] = sx[...]
    rh[z] = sh[...]

    def cut(i, carry):
        rows = pl.ds(pl.multiple_of(i * 64, 64), 64)
        factor_hi[rows, :], factor_lo[rows, :] = split(factor[rows, :], 2)
        return carry

    lax.fori_loop(0, 8, cut, 0)
    norms[...] = row_norms(features[...])
    target = table[pl.ds(pl.multiple_of(z * 32, 32), 32), :][:, :1]
    halves = [target[:16], target[16:]]
    target_x = jnp.concatenate([target * 4 + b for b in range(4)], axis=0)
    target_h = jnp.concatenate(
        [half * 8 + (2 * b + j) for b in range(4) for half in halves for j in range(2)], axis=0
    )
    pick_x = jnp.where(
        lax.broadcasted_iota(jnp.int32, (128, 128), 1) == target_x, 1.0, 0.0
    ).astype(jnp.bfloat16)
    pick_h = jnp.where(
        lax.broadcasted_iota(jnp.int32, (256, 256), 1) == target_h, 1.0, 0.0
    ).astype(jnp.bfloat16)
    for copy in pending:
        copy.wait()
    tx[...] = jnp.dot(
        pick_x, rx[...].reshape(8 * 16, 128), preferred_element_type=jnp.float32
    ).astype(jnp.bfloat16).reshape(4, 2, 16, 128)
    high, low = code_parts(rh[...].reshape(8 * 32, 128))
    picked = 256.0 * jnp.dot(
        pick_h, high.astype(jnp.bfloat16), preferred_element_type=jnp.float32
    ) + jnp.dot(pick_h, low.astype(jnp.bfloat16), preferred_element_type=jnp.float32)
    th[...] = picked.astype(jnp.int32).astype(jnp.int16).reshape(4, 2, 2, 16, 128)

    pending = []
    for i, o in enumerate(XC_PEERS):
        device = peer(**o)
        pending.append(copies.start(tx.at[device[0], device[2]], ax.at[i], device))
        pending.append(copies.start(th.at[device[0], device[2]], ah.at[i], device))
    for copy in pending:
        copy.wait()
    total_x = tx[x, c].astype(jnp.float32)
    total_h = th[x, c].astype(jnp.int32)
    for i in range(7):
        total_x = total_x + ax[i].astype(jnp.float32)
        total_h = total_h + ah[i].astype(jnp.int32)
    bx[...] = total_x.astype(jnp.bfloat16)
    bh[...] = total_h.astype(jnp.int16)

    pending = []
    for i, o in enumerate(Y_PEERS):
        pending.append(copies.start(bx, yx.at[i], peer(**o)))
        pending.append(copies.start(bh, yh.at[i], peer(**o)))
    for copy in pending:
        copy.wait()
    for i in range(7):
        total_x = total_x + yx[i].astype(jnp.float32)
        total_h = total_h + yh[i].astype(jnp.int32)
    fx[c, 0, x] = total_x.astype(jnp.bfloat16)
    fh[c, x, 0] = total_h.astype(jnp.int16)

    x_first = [copies.start(fx.at[c, 0, x], fx.at[c, 0, x], peer(**o)) for o in X_PEERS]
    z_first = [
        copies.start(fh.at[c, x, 0], fh.at[c, x, 7 - i], peer(**o)) for i, o in enumerate(Z_ORDER[::-1])
    ][::-1]
    for copy in x_first:
        copy.wait_recv()
    z_second = [
        copies.start(fx.at[c, 0], fx.at[c, 7 - i], peer(**o)) for i, o in enumerate(Z_ORDER[::-1])
    ][::-1]
    x_second, across = [], []
    for first, size in Z_GROUPS:
        for i in range(max(first, 1), first + size):
            z_first[i - 1].wait_recv()
        part = fh.at[c, x, pl.ds(first, size)]
        for o in X_PEERS:
            x_second.append(copies.start(part, part, peer(**o)))
        across.append(copies.start(part, part, sibling))
    for first, size in Z_GROUPS:
        for i in range(max(first, 1), first + size):
            z_second[i - 1].wait_recv()
        part = fx.at[c, pl.ds(first, size)]
        across.append(copies.start(part, part, sibling))
    for g, (first, size) in enumerate(Z_GROUPS):
        for i, o in list(enumerate(X_PEERS))[::-1]:
            source = lax.rem(x + 4 - o["x"], 4)
            part = fh.at[c, source, pl.ds(first, size)]
            x_second[g * 3 + i].wait_recv()
            across.append(copies.start(part, part, sibling))

    def unpack(core):
        def step(i, carry):
            odd = i % 2
            back = odd * ((i + 1) // 2) + (1 - odd) * (8 - i // 2)
            rows = pl.ds(pl.multiple_of((((z + 8 - back) % 8) * 2 + core) * 16, 16), 16)
            for xb in range(4):
                px[rows, xb * 128 : xb * 128 + 128] = fx[core, i, xb]
                for j in range(2):
                    high, low = code_parts(fh[core, xb, i, j])
                    at = (xb * 2 + j) * 128
                    pa[rows, at : at + 128] = (high * (256.0 / H_SCALE)).astype(jnp.bfloat16)
                    pb[rows, at : at + 128] = (low * (1.0 / H_SCALE)).astype(jnp.bfloat16)
            return carry

        lax.fori_loop(0, 8, step, 0)

    unpack(c)
    for copy in x_first + z_first + z_second + x_second:
        copy.wait_send()
    for copy in across:
        copy.wait()
    unpack(1 - c)

    def local(i, carry):
        span = pl.ds(pl.multiple_of(i * 256, 256), 256)
        h = [factor_hi[span, :], factor_lo[span, :]]
        residual = transposed_kernel(px[...], features[span, :], norms[:, span]) - product(
            [pa[...], pb[...]], h, (1, 1), 2
        )
        rt[i] = residual
        weighted = split(residual * weights[i], 2)
        left = product(weighted, h, (1, 0), 2)
        right = product(weighted, split(residual, 2), (1, 1), 2)
        both = jnp.concatenate([left, right], axis=1)
        for k in range(10):
            m[k] = m[k] + both[:, k * 128 : k * 128 + 128].reshape(4, 8, 8, 128)
        return carry

    m[...] = jnp.zeros_like(m)
    lax.fori_loop(0, 2, local, 0)

    axis_at = dict(x=x, y=y, z=z)
    axis_peers = dict(x=X_PEERS, y=Y_PEERS, z=Z_PEERS)

    class Chunk:
        def __init__(self, o, n, first, second, last, land1, sum1, land2, sum2, land3):
            self.o, self.n = o, n
            self.first, self.second, self.last = first, second, last
            self.land1, self.sum1, self.land2, self.sum2, self.land3 = land1, sum1, land2, sum2, land3
            self.wide = second if first == "x" else first
            self.flying = []

        def line(self, ref, start, along, index):
            block = (pl.ds(start, self.n),)
            return ref.at[block + ((index,) if along == "x" else (slice(None), index))]

        def go(self, pairs):
            self.flying = [copies.start(source, target, device) for source, target, device in pairs]

        def land(self):
            for copy in self.flying:
                copy.wait()

        def targets(self, axis):
            where = AXES.index(axis)
            return [(i, peer(**o)[where], peer(**o)) for i, o in enumerate(axis_peers[axis])]

        def core_out(self):
            theirs = m.at[pl.ds(5 * (1 - c) + self.o, self.n)]
            self.go([(theirs, cl.at[pl.ds(self.o, self.n)], sibling)])

        def first_out(self):
            self.land()
            span = pl.ds(self.o, self.n)
            a1[span] = m[pl.ds(5 * c + self.o, self.n)] + cl[span]
            self.go([
                (self.line(a1, self.o, self.first, at), self.land1.at[i], device)
                for i, at, device in self.targets(self.first)
            ])

        def second_out(self):
            self.land()
            total = self.line(a1, self.o, self.first, axis_at[self.first])[...]
            for i in range(len(axis_peers[self.first])):
                total = total + self.land1[i]
            self.sum1[...] = total
            self.go([
                (self.sum1.at[:, at], self.land2.at[i], device)
                for i, at, device in self.targets(self.second)
            ])

        def last_out(self):
            self.land()
            total = self.sum1[:, axis_at[self.second]]
            for i in range(len(axis_peers[self.second])):
                total = total + self.land2[i]
            self.sum2[...] = total
            here = self.land3.at[axis_at[self.last]]
            here[...] = total
            self.go([(self.sum2, here, device) for _, _, device in self.targets(self.last)])

        def second_back(self):
            self.land()
            total = self.land3[0]
            for i in range(1, 8):
                total = total + self.land3[i]
            block = f.at[pl.ds(5 * c + self.o, self.n), x, axis_at[self.wide]]
            block[...] = total
            self.go([(block, block, device) for _, _, device in self.targets(self.second)])

        def first_back(self):
            self.land()
            block = self.line(f, 5 * c + self.o, self.first, axis_at[self.first])
            self.go([(block, block, device) for _, _, device in self.targets(self.first)])

        def core_back(self):
            if self.first != "x":
                self.land()
                block = f.at[pl.ds(5 * c + self.o, self.n)]
                self.go([(block, block, sibling)])
                return
            sent = self.flying
            block = self.line(f, 5 * c + self.o, "x", x)
            pairs = [copies.start(block, block, sibling)]
            for copy, o in list(zip(sent, X_PEERS))[::-1]:
                copy.wait_recv()
                block = self.line(f, 5 * c + self.o, "x", lax.rem(x + 4 - o["x"], 4))
                pairs.append(copies.start(block, block, sibling))
            for copy in sent:
                copy.wait_send()
            self.flying = pairs

    cx1 = Chunk(0, 2, "x", "z", "y", lx1, sx1, lx2, sx2, lx3)
    cx2 = Chunk(2, 1, "x", "z", "y", mx1, nx1, mx2, nx2, mx3)
    cz = Chunk(3, 1, "z", "x", "y", lz1, sz1, lz2, sz2, lz3)
    cy = Chunk(4, 1, "y", "x", "z", ly1, sy1, ly2, sy2, ly3)

    def begin_block():
        h = [pa[...], pb[...]]
        a[...] = transposed_kernel(px[...], px[...], row_norms(px[...])) - product(h, h, (1, 1), 2)
        row = lax.broadcasted_iota(jnp.int32, (B, B), 0)
        column = lax.broadcasted_iota(jnp.int32, (B, B), 1)
        xi[...] = jnp.where(row == column, 1.0, 0.0)

    def columns_of(i):
        flipped = product(split(xi[...], 3), split(rt[i], 3), (1, 0), 3)
        columns_out[i * 256 : (i + 1) * 256, :] = flipped.T

    for chunk in (cz, cy, cx1, cx2):
        chunk.core_out()
    for chunk in (cz, cy, cx1, cx2):
        chunk.first_out()
    begin_block()
    eliminate(0, 5, a, xi)
    for chunk in (cx1, cz, cy, cx2):
        chunk.second_out()
    eliminate(5, 8, a, xi)
    for chunk in (cz, cy, cx1, cx2):
        chunk.last_out()
    eliminate(8, 16, a, xi)
    for chunk in (cz, cy, cx1, cx2):
        chunk.second_back()
    columns_of(0)
    for chunk in (cz, cy, cx1, cx2):
        chunk.first_back()
    columns_of(1)
    for chunk in (cz, cy, cx1, cx2):
        chunk.core_back()

    inverse = split(xi[...], 3)
    scaled = 1.0 / (512 * 512)

    def applied(*blocks):
        total = jnp.concatenate([f[k].reshape(B, 128) for k in blocks], axis=1)
        return product(inverse, split(total, 3), (1, 0), 3)

    cz.land()
    cy.land()
    gram_out[:, 3 * 128 : 5 * 128] = scaled * applied(3, 4)
    gram_out[:, R:] = scaled * product(split(applied(8, 9), 3), inverse, (1, 1), 3)
    cx1.land()
    gram_out[:, :256] = scaled * applied(0, 1)
    gram_out[:, 5 * 128 : 7 * 128] = scaled * applied(5, 6)
    cx2.land()
    last = scaled * applied(2, 7)
    gram_out[:, 2 * 128 : 3 * 128] = last[:, :128]
    gram_out[:, 7 * 128 : 8 * 128] = last[:, 128:]


def sum_buffers(n, first, second):
    shapes = [
        (first, n, second, 8, 128),
        (n, second, 8, 128),
        (second - 1, n, 8, 128),
        (n, 8, 128),
        (8, n, 8, 128),
    ]
    return [pltpu.VMEM(shape, jnp.float32) for shape in shapes]


def run(features, factor, ip_weights, pivot_owner, pivot_position):
    count = 64 + 16 + 4 * 32
    vmem = pl.BlockSpec(memory_space=pltpu.VMEM)
    hbm = pl.BlockSpec(memory_space=pltpu.HBM)
    f32, bf16, i16 = jnp.float32, jnp.bfloat16, jnp.int16
    return pl.pallas_call(
        whole_kernel,
        out_shape=(
            pltpu.VMEM((512, B), f32),
            pltpu.VMEM((B, R + B), f32),
        ),
        in_specs=[hbm] * 5,
        out_specs=(vmem, vmem),
        scratch_shapes=[
            pltpu.VMEM((1, B), jnp.int32),
            pltpu.VMEM((1, B), jnp.int32),
            pltpu.VMEM((2, 1, 256), f32),
            pltpu.VMEM((512, F), bf16),
            pltpu.VMEM((512, R), f32),
            pltpu.VMEM((512, R), bf16),
            pltpu.VMEM((512, R), bf16),
            pltpu.VMEM((1, 512), f32),
            pltpu.VMEM((B, 128), jnp.int32),
            pltpu.VMEM((16, 128), bf16),
            pltpu.VMEM((32, 128), i16),
            pltpu.VMEM((8, 16, 128), bf16),
            pltpu.VMEM((8, 32, 128), i16),
            pltpu.VMEM((4, 2, 16, 128), bf16),
            pltpu.VMEM((4, 2, 2, 16, 128), i16),
            pltpu.VMEM((7, 16, 128), bf16),
            pltpu.VMEM((7, 2, 16, 128), i16),
            pltpu.VMEM((16, 128), bf16),
            pltpu.VMEM((2, 16, 128), i16),
            pltpu.VMEM((7, 16, 128), bf16),
            pltpu.VMEM((7, 2, 16, 128), i16),
            pltpu.VMEM((2, 8, 4, 16, 128), bf16),
            pltpu.VMEM((2, 4, 8, 2, 16, 128), i16),
            pltpu.VMEM((B, F), bf16),
            pltpu.VMEM((B, R), bf16),
            pltpu.VMEM((B, R), bf16),
            pltpu.VMEM((2, B, 256), f32),
            pltpu.VMEM((10, 4, 8, 8, 128), f32),
            pltpu.VMEM((B, B), f32),
            pltpu.VMEM((B, B), f32),
            pltpu.VMEM((10, 4, 8, 8, 128), f32),
            pltpu.VMEM((5, 4, 8, 8, 128), f32),
            pltpu.VMEM((5, 4, 8, 8, 128), f32),
            *sum_buffers(2, 3, 8),
            *sum_buffers(1, 3, 8),
            *sum_buffers(1, 7, 4),
            *sum_buffers(1, 7, 4),
            pltpu.SemaphoreType.DMA((8,)),
            pltpu.SemaphoreType.DMA((count,)),
            pltpu.SemaphoreType.DMA((count,)),
        ],
        compiler_params=pltpu.CompilerParams(
            collective_id=0, has_side_effects=True, vmem_limit_bytes=48 * 2**20
        ),
    )(
        *(pltpu.with_memory_space_constraint(v, pltpu.HBM) for v in (
            pivot_owner.reshape(1, B), pivot_position.reshape(1, B), ip_weights.reshape(2, 1, 256), features, factor)),
    )


def solution(mesh):
    torus = Mesh(mesh.devices.reshape(4, 8, 2, 8), AXES)
    in_specs = (P(AXES, None), P(AXES, None), P(AXES), P(), P())
    out_specs = (P(AXES, None), P())
    return jax.shard_map(run, mesh=torus, in_specs=in_specs, out_specs=out_specs, check_vma=False)
```

```python
import jax
import jax.numpy as jnp
from jax import lax
from jax.experimental import pallas as pl
from jax.experimental.pallas import tpu as pltpu
from jax.sharding import Mesh
from jax.sharding import PartitionSpec as P

MESH = pl.DeviceIdType.MESH
AXES = ("x", "z", "c", "y")
SIZES = {"x": 4, "z": 8, "c": 2, "y": 8}
F = 512
R = 1024
B = 256
H_SCALE = 2.0**20


def coord(axis):
    return lax.axis_index(axis)


def peer(**offsets):
    return tuple(
        lax.rem(coord(a) + offsets[a] % SIZES[a], SIZES[a]) if a in offsets else coord(a) for a in AXES
    )


class Copies:
    def __init__(self, send_sem, recv_sem):
        self.send_sem, self.recv_sem, self.used = send_sem, recv_sem, 0

    def start(self, src, dst, device):
        copy = pltpu.make_async_remote_copy(
            src_ref=src,
            dst_ref=dst,
            send_sem=self.send_sem.at[self.used],
            recv_sem=self.recv_sem.at[self.used],
            device_id=device,
            device_id_type=MESH,
        )
        self.used += 1
        copy.start()
        return copy


def greet(peers):
    barrier = pltpu.get_barrier_semaphore()
    for device in peers:
        pl.semaphore_signal(barrier, inc=1, device_id=device, device_id_type=MESH)
    return lambda: pl.semaphore_wait(barrier, len(peers))


X_PEERS = [dict(x=d) for d in (2, 1, 3)]
Y_PEERS = [dict(y=d) for d in (4, 3, 5, 2, 6, 1, 7)]
Z_PEERS = [dict(z=d) for d in (4, 3, 5, 2, 6, 1, 7)]
XC_PEERS = [dict(x=d, c=e) for d in (2, 1, 3, 0) for e in (1, 0) if (d, e) != (0, 0)]
Z_ORDER = [dict(z=d) for d in (1, 7, 2, 6, 3, 5, 4)]
CORE = dict(c=1)
Z_GROUPS = ((0, 5), (5, 3))


W = 16


def split(values, count):
    out = []
    for _ in range(count - 1):
        part = values.astype(jnp.bfloat16)
        out.append(part)
        values = values - part.astype(jnp.float32)
    return out + [values.astype(jnp.bfloat16)]


def product(left, right, dims, count):
    order = {2: ((0, 0), (0, 1), (1, 0)), 3: ((0, 0), (0, 1), (1, 0), (0, 2), (2, 0), (1, 1))}[count]
    lhs = jnp.concatenate([left[i] for i, _ in order], axis=dims[0])
    rhs = jnp.concatenate([right[j] for _, j in order], axis=dims[1])
    return lax.dot_general(
        lhs, rhs, (((dims[0],), (dims[1],)), ((), ())), preferred_element_type=jnp.float32
    )


def row_norms(samples):
    ones = jnp.ones((8, F), jnp.bfloat16)
    norms = sum(
        lax.dot_general(ones, s, (((1,), (1,)), ((), ())), preferred_element_type=jnp.float32)
        for s in split(jnp.square(samples.astype(jnp.float32)), 2)
    )
    return norms[0:1]


def transposed_kernel(pivots, samples, norms):
    cross = lax.dot_general(
        pivots, samples, (((1,), (1,)), ((), ())), preferred_element_type=jnp.float32
    )
    pivot_norms = jnp.sum(jnp.square(pivots.astype(jnp.float32)), axis=1, keepdims=True)
    distance = pivot_norms + norms - 2.0 * cross
    quarter = jnp.exp(-(0.25 / F) * distance)
    half = quarter * quarter
    return 0.5 * quarter + 0.3 * half + 0.2 * (half * half)


def pivot_panel(p, base, a, xi):
    first = pl.multiple_of(p * W, W)
    rows = pl.ds(first, W)
    lanes = B - base
    s = a[rows, base:]
    xs = xi[rows, :]
    sub = lax.broadcasted_iota(jnp.int32, (W, 1), 0)
    lane = lax.broadcasted_iota(jnp.int32, (W, lanes), 1) + base
    columns = [
        jnp.sum(jnp.where(lane == first + j, s, 0.0), axis=1, keepdims=True) for j in range(W)
    ]
    pivots = jnp.ones((W, 1), jnp.float32)
    for j in range(W):
        pivot = columns[j][j : j + 1]
        factor = jnp.where(sub > j, columns[j] * (1.0 / pivot), 0.0)
        for k in range(j + 1, W):
            columns[k] = columns[k] - factor * columns[k][j : j + 1]
        s = s - factor * s[j : j + 1]
        xs = xs - factor * xs[j : j + 1]
        pivots = jnp.where(sub == j, pivot, pivots)
    scale = lax.rsqrt(pivots)
    xs = xs * scale
    later = jnp.where(lane >= first + W, s * scale, 0.0)
    update = product(
        split(later, 3), split(jnp.concatenate([later, xs], axis=1), 3), (0, 0), 3
    )
    a[base:, base:] = a[base:, base:] - update[:, :lanes]
    xi[base:, :] = xi[base:, :] - update[:, lanes:]
    xi[rows, :] = xs


def eliminate(first, last, a, xi):
    base = 0 if last * W <= B // 2 else B // 2

    def step(p, carry):
        pivot_panel(p, base, a, xi)
        return carry

    lax.fori_loop(first, last, step, 0)


def code_parts(codes):
    codes = codes.astype(jnp.int32)
    high = (codes + 128) >> 8
    return high.astype(jnp.float32), (codes - high * 256).astype(jnp.float32)


def whole_kernel(
    owner_hbm, position_hbm, weights_hbm, features_hbm, factor_hbm, columns_out, gram_out,
    owner, position, weights, features, factor, factor_hi, factor_lo, norms, table,
    sx, sh, rx, rh, tx, th, ax, ah, bx, bh, yx, yh, fx, fh,
    px, pa, pb, rt, rest_hi, rest_lo, weighted_hi, weighted_lo, m, a, xi, f, cl, a1,
    lx1, sx1, lx2, sx2, lx3, mx1, nx1, mx2, nx2, mx3, lz1, sz1, lz2, sz2, lz3, ly1, sy1, ly2, sy2, ly3,
    load_sem, send_sem, recv_sem,
):
    x, z, c, y = (coord(axis) for axis in AXES)
    copies = Copies(send_sem, recv_sem)
    small = [
        pltpu.make_async_copy(source, target, load_sem.at[5 + i])
        for i, (source, target) in enumerate(
            ((owner_hbm, owner), (position_hbm, position), (weights_hbm, weights))
        )
    ]
    for load in small:
        load.start()
    load_x = pltpu.make_async_copy(features_hbm, features, load_sem.at[0])
    load_x.start()
    loads = []
    for i in range(4):
        rows = pl.ds(i * 128, 128)
        loads.append(
            pltpu.make_async_copy(factor_hbm.at[rows], factor.at[rows], load_sem.at[1 + i])
        )
        loads[i].start()
    wait_for_all = greet([peer(**o) for o in XC_PEERS + Y_PEERS + Z_PEERS])
    sibling = peer(**CORE)

    me = ((x * 8 + z) * 2 + c) * 8 + y
    for load in small:
        load.wait()
    row_owner = owner[...]
    col_owner = jnp.broadcast_to(row_owner.astype(jnp.float32), (B, B)).T.astype(jnp.int32)
    i_row = lax.broadcasted_iota(jnp.int32, (B, B), 0)
    i_col = lax.broadcasted_iota(jnp.int32, (B, B), 1)
    same = col_owner == row_owner
    row_rank = jnp.sum(jnp.where(same & (i_row < i_col), 1.0, 0.0), axis=0, keepdims=True)
    col_rank = jnp.sum(jnp.where(same & (i_col < i_row), 1.0, 0.0), axis=1, keepdims=True)
    near = col_owner[:, :128] // 128 == x
    near = near & (col_owner[:, :128] % 8 == y) & ((col_owner[:, :128] // 8) % 2 == c)
    place = (col_owner[:, :128] // 16) % 8 * 4 + col_rank.astype(jnp.int32)
    table[...] = jnp.where(near, place, -64)

    order = row_rank.astype(jnp.int32)
    spots = [
        jnp.sum(jnp.where((row_owner == me) & (order == s), position[...], 0)) for s in range(4)
    ]
    slot = lax.broadcasted_iota(jnp.int32, (16, 512), 0) // 4
    lane = lax.broadcasted_iota(jnp.int32, (16, 512), 1)
    wanted = jnp.where(slot == 0, spots[0], jnp.where(slot == 1, spots[1], jnp.where(slot == 2, spots[2], spots[3])))
    pick = jnp.where(lane == wanted, 1.0, 0.0).astype(jnp.bfloat16)
    load_x.wait()
    rows_x = jnp.dot(pick, features[...], preferred_element_type=jnp.float32)
    block_x = lax.broadcasted_iota(jnp.int32, (16, 128), 0) % 4
    sx[...] = sum(
        jnp.where(block_x == b, rows_x[:, b * 128 : b * 128 + 128], 0.0) for b in range(4)
    ).astype(jnp.bfloat16)
    for load in loads:
        load.wait()
    rows_h = [factor[pl.ds(spot, 1), :] for spot in spots]
    own_h = jnp.concatenate(
        [row[:, b * 128 : b * 128 + 128] for row in rows_h for b in range(8)], axis=0
    )
    sh[...] = jnp.round(own_h * H_SCALE).astype(jnp.int32).astype(jnp.int16)

    wait_for_all()
    pending = []
    for o in Z_PEERS:
        pending.append(copies.start(sx, rx.at[z], peer(**o)))
        pending.append(copies.start(sh, rh.at[z], peer(**o)))
    rx[z] = sx[...]
    rh[z] = sh[...]

    def cut(i, carry):
        rows = pl.ds(pl.multiple_of(i * 64, 64), 64)
        factor_hi[rows, :], factor_lo[rows, :] = split(factor[rows, :], 2)
        return carry

    lax.fori_loop(0, 8, cut, 0)
    norms[...] = row_norms(features[...])
    target = table[pl.ds(pl.multiple_of(z * 32, 32), 32), :][:, :1]
    halves = [target[:16], target[16:]]
    target_x = jnp.concatenate([target * 4 + b for b in range(4)], axis=0)
    target_h = jnp.concatenate(
        [half * 8 + (2 * b + j) for b in range(4) for half in halves for j in range(2)], axis=0
    )
    pick_x = jnp.where(
        lax.broadcasted_iota(jnp.int32, (128, 128), 1) == target_x, 1.0, 0.0
    ).astype(jnp.bfloat16)
    pick_h = jnp.where(
        lax.broadcasted_iota(jnp.int32, (256, 256), 1) == target_h, 1.0, 0.0
    ).astype(jnp.bfloat16)
    for copy in pending:
        copy.wait()
    tx[...] = jnp.dot(
        pick_x, rx[...].reshape(8 * 16, 128), preferred_element_type=jnp.float32
    ).astype(jnp.bfloat16).reshape(4, 2, 16, 128)
    high, low = code_parts(rh[...].reshape(8 * 32, 128))
    picked = 256.0 * jnp.dot(
        pick_h, high.astype(jnp.bfloat16), preferred_element_type=jnp.float32
    ) + jnp.dot(pick_h, low.astype(jnp.bfloat16), preferred_element_type=jnp.float32)
    th[...] = picked.astype(jnp.int32).astype(jnp.int16).reshape(4, 2, 2, 16, 128)

    pending = []
    for i, o in enumerate(XC_PEERS):
        device = peer(**o)
        pending.append(copies.start(tx.at[device[0], device[2]], ax.at[i], device))
        pending.append(copies.start(th.at[device[0], device[2]], ah.at[i], device))
    for copy in pending:
        copy.wait()
    total_x = tx[x, c].astype(jnp.float32)
    total_h = th[x, c].astype(jnp.int32)
    for i in range(7):
        total_x = total_x + ax[i].astype(jnp.float32)
        total_h = total_h + ah[i].astype(jnp.int32)
    bx[...] = total_x.astype(jnp.bfloat16)
    bh[...] = total_h.astype(jnp.int16)

    pending = []
    for i, o in enumerate(Y_PEERS):
        pending.append(copies.start(bx, yx.at[i], peer(**o)))
        pending.append(copies.start(bh, yh.at[i], peer(**o)))
    for copy in pending:
        copy.wait()
    for i in range(7):
        total_x = total_x + yx[i].astype(jnp.float32)
        total_h = total_h + yh[i].astype(jnp.int32)
    fx[c, 0, x] = total_x.astype(jnp.bfloat16)
    fh[c, x, 0] = total_h.astype(jnp.int16)

    x_first = [copies.start(fx.at[c, 0, x], fx.at[c, 0, x], peer(**o)) for o in X_PEERS]
    z_first = [
        copies.start(fh.at[c, x, 0], fh.at[c, x, 7 - i], peer(**o)) for i, o in enumerate(Z_ORDER[::-1])
    ][::-1]
    for copy in x_first:
        copy.wait_recv()
    z_second = [
        copies.start(fx.at[c, 0], fx.at[c, 7 - i], peer(**o)) for i, o in enumerate(Z_ORDER[::-1])
    ][::-1]
    x_second, across = [], []
    for first, size in Z_GROUPS:
        for i in range(max(first, 1), first + size):
            z_first[i - 1].wait_recv()
        part = fh.at[c, x, pl.ds(first, size)]
        for o in X_PEERS:
            x_second.append(copies.start(part, part, peer(**o)))
        across.append(copies.start(part, part, sibling))
    for first, size in Z_GROUPS:
        for i in range(max(first, 1), first + size):
            z_second[i - 1].wait_recv()
        part = fx.at[c, pl.ds(first, size)]
        across.append(copies.start(part, part, sibling))
    for g, (first, size) in enumerate(Z_GROUPS):
        for i, o in list(enumerate(X_PEERS))[::-1]:
            source = lax.rem(x + 4 - o["x"], 4)
            part = fh.at[c, source, pl.ds(first, size)]
            x_second[g * 3 + i].wait_recv()
            across.append(copies.start(part, part, sibling))

    def unpack(core):
        def step(i, carry):
            odd = i % 2
            back = odd * ((i + 1) // 2) + (1 - odd) * (8 - i // 2)
            rows = pl.ds(pl.multiple_of((((z + 8 - back) % 8) * 2 + core) * 16, 16), 16)
            for xb in range(4):
                px[rows, xb * 128 : xb * 128 + 128] = fx[core, i, xb]
                for j in range(2):
                    high, low = code_parts(fh[core, xb, i, j])
                    at = (xb * 2 + j) * 128
                    pa[rows, at : at + 128] = (high * (256.0 / H_SCALE)).astype(jnp.bfloat16)
                    pb[rows, at : at + 128] = (low * (1.0 / H_SCALE)).astype(jnp.bfloat16)
            return carry

        lax.fori_loop(0, 8, step, 0)

    unpack(c)
    for copy in x_first + z_first + z_second + x_second:
        copy.wait_send()
    for copy in across:
        copy.wait()
    unpack(1 - c)

    def local(i, carry):
        span = pl.ds(pl.multiple_of(i * 256, 256), 256)
        h = [factor_hi[span, :], factor_lo[span, :]]
        residual = transposed_kernel(px[...], features[span, :], norms[:, span]) - product(
            [pa[...], pb[...]], h, (1, 1), 2
        )
        rt[i] = residual
        rest_hi[:, span], rest_lo[:, span] = split(residual, 2)
        weighted_hi[:, span], weighted_lo[:, span] = split(residual * weights[i], 2)
        return carry

    lax.fori_loop(0, 2, local, 0)

    def share(half):
        weighted = [weighted_hi[...], weighted_lo[...]]
        lanes = slice(0, 640) if half == 0 else slice(640, R)
        values = product(weighted, [factor_hi[:, lanes], factor_lo[:, lanes]], (1, 0), 2)
        if half == 1:
            right = product(weighted, [rest_hi[...], rest_lo[...]], (1, 1), 2)
            values = jnp.concatenate([values, right], axis=1)
        for k in range(5):
            m[5 * half + k] = values[:, k * 128 : k * 128 + 128].reshape(4, 8, 8, 128)

    def share_when(core, half):
        pl.when(c == core)(lambda: share(half))

    share_when(0, 1)
    share_when(1, 0)

    axis_at = dict(x=x, y=y, z=z)
    axis_peers = dict(x=X_PEERS, y=Y_PEERS, z=Z_PEERS)

    class Chunk:
        def __init__(self, o, n, first, second, last, land1, sum1, land2, sum2, land3):
            self.o, self.n = o, n
            self.first, self.second, self.last = first, second, last
            self.land1, self.sum1, self.land2, self.sum2, self.land3 = land1, sum1, land2, sum2, land3
            self.wide = second if first == "x" else first
            self.flying = []

        def line(self, ref, start, along, index):
            block = (pl.ds(start, self.n),)
            return ref.at[block + ((index,) if along == "x" else (slice(None), index))]

        def go(self, pairs):
            self.flying = [copies.start(source, target, device) for source, target, device in pairs]

        def land(self):
            for copy in self.flying:
                copy.wait()

        def targets(self, axis):
            where = AXES.index(axis)
            return [(i, peer(**o)[where], peer(**o)) for i, o in enumerate(axis_peers[axis])]

        def core_out(self):
            theirs = m.at[pl.ds(5 * (1 - c) + self.o, self.n)]
            self.go([(theirs, cl.at[pl.ds(self.o, self.n)], sibling)])

        def first_out(self):
            self.land()
            span = pl.ds(self.o, self.n)
            a1[span] = m[pl.ds(5 * c + self.o, self.n)] + cl[span]
            self.go([
                (self.line(a1, self.o, self.first, at), self.land1.at[i], device)
                for i, at, device in self.targets(self.first)
            ])

        def second_out(self):
            self.land()
            total = self.line(a1, self.o, self.first, axis_at[self.first])[...]
            for i in range(len(axis_peers[self.first])):
                total = total + self.land1[i]
            self.sum1[...] = total
            self.go([
                (self.sum1.at[:, at], self.land2.at[i], device)
                for i, at, device in self.targets(self.second)
            ])

        def last_out(self):
            self.land()
            total = self.sum1[:, axis_at[self.second]]
            for i in range(len(axis_peers[self.second])):
                total = total + self.land2[i]
            self.sum2[...] = total
            here = self.land3.at[axis_at[self.last]]
            here[...] = total
            self.go([(self.sum2, here, device) for _, _, device in self.targets(self.last)])

        def second_back(self):
            self.land()
            total = self.land3[0]
            for i in range(1, 8):
                total = total + self.land3[i]
            block = f.at[pl.ds(5 * c + self.o, self.n), x, axis_at[self.wide]]
            block[...] = total
            self.go([(block, block, device) for _, _, device in self.targets(self.second)])

        def first_back(self):
            self.land()
            block = self.line(f, 5 * c + self.o, self.first, axis_at[self.first])
            self.go([(block, block, device) for _, _, device in self.targets(self.first)])

        def core_back(self):
            if self.first != "x":
                self.land()
                block = f.at[pl.ds(5 * c + self.o, self.n)]
                self.go([(block, block, sibling)])
                return
            sent = self.flying
            block = self.line(f, 5 * c + self.o, "x", x)
            pairs = [copies.start(block, block, sibling)]
            for copy, o in list(zip(sent, X_PEERS))[::-1]:
                copy.wait_recv()
                block = self.line(f, 5 * c + self.o, "x", lax.rem(x + 4 - o["x"], 4))
                pairs.append(copies.start(block, block, sibling))
            for copy in sent:
                copy.wait_send()
            self.flying = pairs

    cx1 = Chunk(0, 2, "x", "z", "y", lx1, sx1, lx2, sx2, lx3)
    cx2 = Chunk(2, 1, "x", "z", "y", mx1, nx1, mx2, nx2, mx3)
    cz = Chunk(3, 1, "z", "x", "y", lz1, sz1, lz2, sz2, lz3)
    cy = Chunk(4, 1, "y", "x", "z", ly1, sy1, ly2, sy2, ly3)

    def begin_block():
        h = [pa[...], pb[...]]
        a[...] = transposed_kernel(px[...], px[...], row_norms(px[...])) - product(h, h, (1, 1), 2)
        row = lax.broadcasted_iota(jnp.int32, (B, B), 0)
        column = lax.broadcasted_iota(jnp.int32, (B, B), 1)
        xi[...] = jnp.where(row == column, 1.0, 0.0)

    def columns_of(i):
        flipped = product(split(xi[...], 3), split(rt[i], 3), (1, 0), 3)
        columns_out[i * 256 : (i + 1) * 256, :] = flipped.T

    for chunk in (cz, cy, cx1, cx2):
        chunk.core_out()
    share_when(0, 0)
    share_when(1, 1)
    for chunk in (cz, cy, cx1, cx2):
        chunk.first_out()
    begin_block()
    eliminate(0, 5, a, xi)
    for chunk in (cx1, cz, cy, cx2):
        chunk.second_out()
    eliminate(5, 8, a, xi)
    for chunk in (cz, cy, cx1, cx2):
        chunk.last_out()
    eliminate(8, 16, a, xi)
    for chunk in (cz, cy, cx1, cx2):
        chunk.second_back()
    columns_of(0)
    for chunk in (cz, cy, cx1, cx2):
        chunk.first_back()
    columns_of(1)
    for chunk in (cz, cy, cx1, cx2):
        chunk.core_back()

    inverse = split(xi[...], 3)
    scaled = 1.0 / (512 * 512)

    def applied(*blocks):
        total = jnp.concatenate([f[k].reshape(B, 128) for k in blocks], axis=1)
        return product(inverse, split(total, 3), (1, 0), 3)

    cz.land()
    cy.land()
    gram_out[:, 3 * 128 : 5 * 128] = scaled * applied(3, 4)
    gram_out[:, R:] = scaled * product(split(applied(8, 9), 3), inverse, (1, 1), 3)
    cx1.land()
    gram_out[:, :256] = scaled * applied(0, 1)
    gram_out[:, 5 * 128 : 7 * 128] = scaled * applied(5, 6)
    cx2.land()
    last = scaled * applied(2, 7)
    gram_out[:, 2 * 128 : 3 * 128] = last[:, :128]
    gram_out[:, 7 * 128 : 8 * 128] = last[:, 128:]


def sum_buffers(n, first, second):
    shapes = [
        (first, n, second, 8, 128),
        (n, second, 8, 128),
        (second - 1, n, 8, 128),
        (n, 8, 128),
        (8, n, 8, 128),
    ]
    return [pltpu.VMEM(shape, jnp.float32) for shape in shapes]


def run(features, factor, ip_weights, pivot_owner, pivot_position):
    count = 64 + 16 + 4 * 32
    vmem = pl.BlockSpec(memory_space=pltpu.VMEM)
    hbm = pl.BlockSpec(memory_space=pltpu.HBM)
    f32, bf16, i16 = jnp.float32, jnp.bfloat16, jnp.int16
    results = pl.pallas_call(
        whole_kernel,
        out_shape=(
            pltpu.VMEM((512, B), f32),
            pltpu.VMEM((B, R + B), f32),
        ),
        in_specs=[hbm] * 5,
        out_specs=(vmem, vmem),
        scratch_shapes=[
            pltpu.VMEM((1, B), jnp.int32),
            pltpu.VMEM((1, B), jnp.int32),
            pltpu.VMEM((2, 1, 256), f32),
            pltpu.VMEM((512, F), bf16),
            pltpu.VMEM((512, R), f32),
            pltpu.VMEM((512, R), bf16),
            pltpu.VMEM((512, R), bf16),
            pltpu.VMEM((1, 512), f32),
            pltpu.VMEM((B, 128), jnp.int32),
            pltpu.VMEM((16, 128), bf16),
            pltpu.VMEM((32, 128), i16),
            pltpu.VMEM((8, 16, 128), bf16),
            pltpu.VMEM((8, 32, 128), i16),
            pltpu.VMEM((4, 2, 16, 128), bf16),
            pltpu.VMEM((4, 2, 2, 16, 128), i16),
            pltpu.VMEM((7, 16, 128), bf16),
            pltpu.VMEM((7, 2, 16, 128), i16),
            pltpu.VMEM((16, 128), bf16),
            pltpu.VMEM((2, 16, 128), i16),
            pltpu.VMEM((7, 16, 128), bf16),
            pltpu.VMEM((7, 2, 16, 128), i16),
            pltpu.VMEM((2, 8, 4, 16, 128), bf16),
            pltpu.VMEM((2, 4, 8, 2, 16, 128), i16),
            pltpu.VMEM((B, F), bf16),
            pltpu.VMEM((B, R), bf16),
            pltpu.VMEM((B, R), bf16),
            pltpu.VMEM((2, B, 256), f32),
            pltpu.VMEM((B, 512), bf16),
            pltpu.VMEM((B, 512), bf16),
            pltpu.VMEM((B, 512), bf16),
            pltpu.VMEM((B, 512), bf16),
            pltpu.VMEM((10, 4, 8, 8, 128), f32),
            pltpu.VMEM((B, B), f32),
            pltpu.VMEM((B, B), f32),
            pltpu.VMEM((10, 4, 8, 8, 128), f32),
            pltpu.VMEM((5, 4, 8, 8, 128), f32),
            pltpu.VMEM((5, 4, 8, 8, 128), f32),
            *sum_buffers(2, 3, 8),
            *sum_buffers(1, 3, 8),
            *sum_buffers(1, 7, 4),
            *sum_buffers(1, 7, 4),
            pltpu.SemaphoreType.DMA((8,)),
            pltpu.SemaphoreType.DMA((count,)),
            pltpu.SemaphoreType.DMA((count,)),
        ],
        compiler_params=pltpu.CompilerParams(
            collective_id=0, has_side_effects=True, vmem_limit_bytes=48 * 2**20
        ),
    )(
        *(pltpu.with_memory_space_constraint(v, pltpu.HBM) for v in (
            pivot_owner.reshape(1, B), pivot_position.reshape(1, B), ip_weights.reshape(2, 1, 256), features, factor)),
    )
    vmem = pl.BlockSpec(memory_space=pltpu.VMEM)
    return pl.pallas_call(
        write_kernel,
        out_shape=(pltpu.HBM((512, B), f32), pltpu.HBM((B, R + B), f32)),
        in_specs=[vmem, vmem],
        out_specs=(hbm, hbm),
        scratch_shapes=[pltpu.SemaphoreType.DMA((3,))],
        compiler_params=pltpu.CompilerParams(vmem_limit_bytes=2**20),
    )(*results)


def write_kernel(columns, gram, columns_out, gram_out, sem):
    copies = [
        pltpu.make_async_copy(columns, columns_out, sem.at[0]),
        pltpu.make_async_copy(gram.at[pl.ds(0, 128)], gram_out.at[pl.ds(0, 128)], sem.at[1]),
        pltpu.make_async_copy(gram.at[pl.ds(128, 128)], gram_out.at[pl.ds(128, 128)], sem.at[2]),
    ]
    for copy in copies:
        copy.start()
    for copy in copies:
        copy.wait()


def solution(mesh):
    torus = Mesh(mesh.devices.reshape(4, 8, 2, 8), AXES)
    in_specs = (P(AXES, None), P(AXES, None), P(AXES), P(), P())
    out_specs = (P(AXES, None), P())
    return jax.shard_map(run, mesh=torus, in_specs=in_specs, out_specs=out_specs, check_vma=False)
```

```python
import jax
import jax.numpy as jnp
from jax import lax
from jax.experimental import pallas as pl
from jax.experimental.pallas import tpu as pltpu
from jax.sharding import Mesh
from jax.sharding import PartitionSpec as P

MESH = pl.DeviceIdType.MESH
AXES = ("x", "z", "c", "y")
SIZES = {"x": 4, "z": 8, "c": 2, "y": 8}
F = 512
R = 1024
B = 256
H_SCALE = 2.0**20


def coord(axis):
    return lax.axis_index(axis)


def peer(**offsets):
    return tuple(
        lax.rem(coord(a) + offsets[a] % SIZES[a], SIZES[a]) if a in offsets else coord(a) for a in AXES
    )


class Copies:
    def __init__(self, send_sem, recv_sem):
        self.send_sem, self.recv_sem, self.used = send_sem, recv_sem, 0

    def start(self, src, dst, device):
        copy = pltpu.make_async_remote_copy(
            src_ref=src,
            dst_ref=dst,
            send_sem=self.send_sem.at[self.used],
            recv_sem=self.recv_sem.at[self.used],
            device_id=device,
            device_id_type=MESH,
        )
        self.used += 1
        copy.start()
        return copy


def greet(peers):
    barrier = pltpu.get_barrier_semaphore()
    for device in peers:
        pl.semaphore_signal(barrier, inc=1, device_id=device, device_id_type=MESH)
    return lambda: pl.semaphore_wait(barrier, len(peers))


X_PEERS = [dict(x=d) for d in (2, 1, 3)]
Y_PEERS = [dict(y=d) for d in (4, 3, 5, 2, 6, 1, 7)]
Z_PEERS = [dict(z=d) for d in (4, 3, 5, 2, 6, 1, 7)]
XC_PEERS = [dict(x=d, c=e) for d in (2, 1, 3, 0) for e in (1, 0) if (d, e) != (0, 0)]
Z_ORDER = [dict(z=d) for d in (1, 7, 2, 6, 3, 5, 4)]
CORE = dict(c=1)
Z_GROUPS = ((0, 5), (5, 3))


W = 16


def split(values, count):
    out = []
    for _ in range(count - 1):
        part = values.astype(jnp.bfloat16)
        out.append(part)
        values = values - part.astype(jnp.float32)
    return out + [values.astype(jnp.bfloat16)]


def product(left, right, dims, count):
    order = {2: ((0, 0), (0, 1), (1, 0)), 3: ((0, 0), (0, 1), (1, 0), (0, 2), (2, 0), (1, 1))}[count]
    lhs = jnp.concatenate([left[i] for i, _ in order], axis=dims[0])
    rhs = jnp.concatenate([right[j] for _, j in order], axis=dims[1])
    return lax.dot_general(
        lhs, rhs, (((dims[0],), (dims[1],)), ((), ())), preferred_element_type=jnp.float32
    )


def row_norms(samples):
    ones = jnp.ones((8, F), jnp.bfloat16)
    norms = sum(
        lax.dot_general(ones, s, (((1,), (1,)), ((), ())), preferred_element_type=jnp.float32)
        for s in split(jnp.square(samples.astype(jnp.float32)), 2)
    )
    return norms[0:1]


def transposed_kernel(pivots, samples, norms):
    cross = lax.dot_general(
        pivots, samples, (((1,), (1,)), ((), ())), preferred_element_type=jnp.float32
    )
    pivot_norms = jnp.sum(jnp.square(pivots.astype(jnp.float32)), axis=1, keepdims=True)
    distance = pivot_norms + norms - 2.0 * cross
    quarter = jnp.exp(-(0.25 / F) * distance)
    half = quarter * quarter
    return 0.5 * quarter + 0.3 * half + 0.2 * (half * half)


def pivot_panel(p, base, a, xi):
    first = pl.multiple_of(p * W, W)
    rows = pl.ds(first, W)
    lanes = B - base
    s = a[rows, base:]
    xs = xi[rows, :]
    sub = lax.broadcasted_iota(jnp.int32, (W, 1), 0)
    lane = lax.broadcasted_iota(jnp.int32, (W, lanes), 1) + base
    columns = [
        jnp.sum(jnp.where(lane == first + j, s, 0.0), axis=1, keepdims=True) for j in range(W)
    ]
    pivots = jnp.ones((W, 1), jnp.float32)
    for j in range(W):
        pivot = columns[j][j : j + 1]
        factor = jnp.where(sub > j, columns[j] * (1.0 / pivot), 0.0)
        for k in range(j + 1, W):
            columns[k] = columns[k] - factor * columns[k][j : j + 1]
        s = s - factor * s[j : j + 1]
        xs = xs - factor * xs[j : j + 1]
        pivots = jnp.where(sub == j, pivot, pivots)
    scale = lax.rsqrt(pivots)
    xs = xs * scale
    later = jnp.where(lane >= first + W, s * scale, 0.0)
    update = product(
        split(later, 3), split(jnp.concatenate([later, xs], axis=1), 3), (0, 0), 3
    )
    a[base:, base:] = a[base:, base:] - update[:, :lanes]
    xi[base:, :] = xi[base:, :] - update[:, lanes:]
    xi[rows, :] = xs


def eliminate(first, last, a, xi):
    base = 0 if last * W <= B // 2 else B // 2

    def step(p, carry):
        pivot_panel(p, base, a, xi)
        return carry

    lax.fori_loop(first, last, step, 0)


def code_parts(codes):
    codes = codes.astype(jnp.int32)
    high = (codes + 128) >> 8
    return high.astype(jnp.float32), (codes - high * 256).astype(jnp.float32)


def whole_kernel(
    owner_hbm, position_hbm, weights_hbm, features_hbm, factor_hbm, columns_out, gram_out,
    owner, position, weights, features, factor, factor_hi, factor_lo, norms, table,
    sx, sh, rx, rh, tx, th, ax, ah, bx, bh, yx, yh, fx, fh,
    px, pa, pb, rt, rest_hi, rest_lo, weighted_hi, weighted_lo, m, a, xi, f, cl, a1,
    lx1, sx1, lx2, sx2, lx3, mx1, nx1, mx2, nx2, mx3, lz1, sz1, lz2, sz2, lz3, ly1, sy1, ly2, sy2, ly3,
    load_sem, send_sem, recv_sem,
):
    x, z, c, y = (coord(axis) for axis in AXES)
    copies = Copies(send_sem, recv_sem)
    wait_for_all = greet([peer(**o) for o in Z_PEERS + Y_PEERS + XC_PEERS])
    small = [
        pltpu.make_async_copy(source, target, load_sem.at[5 + i])
        for i, (source, target) in enumerate(
            ((owner_hbm, owner), (position_hbm, position), (weights_hbm, weights))
        )
    ]
    for load in small:
        load.start()
    load_x = pltpu.make_async_copy(features_hbm, features, load_sem.at[0])
    load_x.start()
    loads = []
    for i in range(4):
        rows = pl.ds(i * 128, 128)
        loads.append(
            pltpu.make_async_copy(factor_hbm.at[rows], factor.at[rows], load_sem.at[1 + i])
        )
        loads[i].start()
    sibling = peer(**CORE)

    me = ((x * 8 + z) * 2 + c) * 8 + y
    for load in small:
        load.wait()
    row_owner = owner[...]
    col_owner = jnp.broadcast_to(row_owner.astype(jnp.float32), (B, B)).T.astype(jnp.int32)
    i_row = lax.broadcasted_iota(jnp.int32, (B, B), 0)
    i_col = lax.broadcasted_iota(jnp.int32, (B, B), 1)
    same = col_owner == row_owner
    row_rank = jnp.sum(jnp.where(same & (i_row < i_col), 1.0, 0.0), axis=0, keepdims=True)
    col_rank = jnp.sum(jnp.where(same & (i_col < i_row), 1.0, 0.0), axis=1, keepdims=True)
    near = col_owner[:, :128] // 128 == x
    near = near & (col_owner[:, :128] % 8 == y) & ((col_owner[:, :128] // 8) % 2 == c)
    place = (col_owner[:, :128] // 16) % 8 * 4 + col_rank.astype(jnp.int32)
    table[...] = jnp.where(near, place, -64)

    order = row_rank.astype(jnp.int32)
    spots = [
        jnp.sum(jnp.where((row_owner == me) & (order == s), position[...], 0)) for s in range(4)
    ]
    slot = lax.broadcasted_iota(jnp.int32, (16, 512), 0) // 4
    lane = lax.broadcasted_iota(jnp.int32, (16, 512), 1)
    wanted = jnp.where(slot == 0, spots[0], jnp.where(slot == 1, spots[1], jnp.where(slot == 2, spots[2], spots[3])))
    pick = jnp.where(lane == wanted, 1.0, 0.0).astype(jnp.bfloat16)
    load_x.wait()
    rows_x = jnp.dot(pick, features[...], preferred_element_type=jnp.float32)
    block_x = lax.broadcasted_iota(jnp.int32, (16, 128), 0) % 4
    sx[...] = sum(
        jnp.where(block_x == b, rows_x[:, b * 128 : b * 128 + 128], 0.0) for b in range(4)
    ).astype(jnp.bfloat16)
    for load in loads:
        load.wait()
    rows_h = [factor[pl.ds(spot, 1), :] for spot in spots]
    own_h = jnp.concatenate(
        [row[:, b * 128 : b * 128 + 128] for row in rows_h for b in range(8)], axis=0
    )
    sh[...] = jnp.round(own_h * H_SCALE).astype(jnp.int32).astype(jnp.int16)

    wait_for_all()
    pending = []
    for o in Z_PEERS:
        pending.append(copies.start(sx, rx.at[z], peer(**o)))
        pending.append(copies.start(sh, rh.at[z], peer(**o)))
    rx[z] = sx[...]
    rh[z] = sh[...]

    def cut(i, carry):
        rows = pl.ds(pl.multiple_of(i * 64, 64), 64)
        factor_hi[rows, :], factor_lo[rows, :] = split(factor[rows, :], 2)
        return carry

    lax.fori_loop(0, 8, cut, 0)
    norms[...] = row_norms(features[...])
    target = table[pl.ds(pl.multiple_of(z * 32, 32), 32), :][:, :1]
    halves = [target[:16], target[16:]]
    target_x = jnp.concatenate([target * 4 + b for b in range(4)], axis=0)
    target_h = jnp.concatenate(
        [half * 8 + (2 * b + j) for b in range(4) for half in halves for j in range(2)], axis=0
    )
    pick_x = jnp.where(
        lax.broadcasted_iota(jnp.int32, (128, 128), 1) == target_x, 1.0, 0.0
    ).astype(jnp.bfloat16)
    pick_h = jnp.where(
        lax.broadcasted_iota(jnp.int32, (256, 256), 1) == target_h, 1.0, 0.0
    ).astype(jnp.bfloat16)
    for copy in pending[::-1]:
        copy.wait()
    tx[...] = jnp.dot(
        pick_x, rx[...].reshape(8 * 16, 128), preferred_element_type=jnp.float32
    ).astype(jnp.bfloat16).reshape(4, 2, 16, 128)
    high, low = code_parts(rh[...].reshape(8 * 32, 128))
    picked = 256.0 * jnp.dot(
        pick_h, high.astype(jnp.bfloat16), preferred_element_type=jnp.float32
    ) + jnp.dot(pick_h, low.astype(jnp.bfloat16), preferred_element_type=jnp.float32)
    th[...] = picked.astype(jnp.int32).astype(jnp.int16).reshape(4, 2, 2, 16, 128)

    pending = []
    for i, o in enumerate(XC_PEERS):
        device = peer(**o)
        pending.append(copies.start(tx.at[device[0], device[2]], ax.at[i], device))
        pending.append(copies.start(th.at[device[0], device[2]], ah.at[i], device))
    for copy in pending[::-1]:
        copy.wait()
    total_x = tx[x, c].astype(jnp.float32)
    total_h = th[x, c].astype(jnp.int32)
    for i in range(7):
        total_x = total_x + ax[i].astype(jnp.float32)
        total_h = total_h + ah[i].astype(jnp.int32)
    bx[...] = total_x.astype(jnp.bfloat16)
    bh[...] = total_h.astype(jnp.int16)

    pending = []
    for i, o in enumerate(Y_PEERS):
        pending.append(copies.start(bx, yx.at[i], peer(**o)))
        pending.append(copies.start(bh, yh.at[i], peer(**o)))
    for copy in pending[::-1]:
        copy.wait()
    for i in range(7):
        total_x = total_x + yx[i].astype(jnp.float32)
        total_h = total_h + yh[i].astype(jnp.int32)
    fx[c, 0, x] = total_x.astype(jnp.bfloat16)
    fh[c, x, 0] = total_h.astype(jnp.int16)

    x_first = [copies.start(fx.at[c, 0, x], fx.at[c, 0, x], peer(**o)) for o in X_PEERS]
    z_first = [
        copies.start(fh.at[c, x, 0], fh.at[c, x, 7 - i], peer(**o)) for i, o in enumerate(Z_ORDER[::-1])
    ][::-1]
    for copy in x_first:
        copy.wait_recv()
    z_second = [
        copies.start(fx.at[c, 0], fx.at[c, 7 - i], peer(**o)) for i, o in enumerate(Z_ORDER[::-1])
    ][::-1]
    x_second, across = [], []
    for first, size in Z_GROUPS:
        for i in range(max(first, 1), first + size):
            z_first[i - 1].wait_recv()
        part = fh.at[c, x, pl.ds(first, size)]
        for o in X_PEERS:
            x_second.append(copies.start(part, part, peer(**o)))
        across.append(copies.start(part, part, sibling))
    for first, size in Z_GROUPS:
        for i in range(max(first, 1), first + size):
            z_second[i - 1].wait_recv()
        part = fx.at[c, pl.ds(first, size)]
        across.append(copies.start(part, part, sibling))
    for g, (first, size) in enumerate(Z_GROUPS):
        for i, o in list(enumerate(X_PEERS))[::-1]:
            source = lax.rem(x + 4 - o["x"], 4)
            part = fh.at[c, source, pl.ds(first, size)]
            x_second[g * 3 + i].wait_recv()
            across.append(copies.start(part, part, sibling))

    def unpack(core):
        def step(i, carry):
            odd = i % 2
            back = odd * ((i + 1) // 2) + (1 - odd) * (8 - i // 2)
            rows = pl.ds(pl.multiple_of((((z + 8 - back) % 8) * 2 + core) * 16, 16), 16)
            for xb in range(4):
                px[rows, xb * 128 : xb * 128 + 128] = fx[core, i, xb]
                for j in range(2):
                    high, low = code_parts(fh[core, xb, i, j])
                    at = (xb * 2 + j) * 128
                    pa[rows, at : at + 128] = (high * (256.0 / H_SCALE)).astype(jnp.bfloat16)
                    pb[rows, at : at + 128] = (low * (1.0 / H_SCALE)).astype(jnp.bfloat16)
            return carry

        lax.fori_loop(0, 8, step, 0)

    unpack(c)
    for copy in x_first + z_first + z_second + x_second:
        copy.wait_send()
    for copy in across:
        copy.wait()
    unpack(1 - c)

    def local(i, carry):
        span = pl.ds(pl.multiple_of(i * 256, 256), 256)
        h = [factor_hi[span, :], factor_lo[span, :]]
        residual = transposed_kernel(px[...], features[span, :], norms[:, span]) - product(
            [pa[...], pb[...]], h, (1, 1), 2
        )
        rt[i] = residual
        rest_hi[:, span], rest_lo[:, span] = split(residual, 2)
        weighted_hi[:, span], weighted_lo[:, span] = split(residual * weights[i], 2)
        return carry

    lax.fori_loop(0, 2, local, 0)

    def share(half):
        weighted = [weighted_hi[...], weighted_lo[...]]
        lanes = slice(0, 640) if half == 0 else slice(640, R)
        values = product(weighted, [factor_hi[:, lanes], factor_lo[:, lanes]], (1, 0), 2)
        if half == 1:
            right = product(weighted, [rest_hi[...], rest_lo[...]], (1, 1), 2)
            values = jnp.concatenate([values, right], axis=1)
        for k in range(5):
            m[5 * half + k] = values[:, k * 128 : k * 128 + 128].reshape(4, 8, 8, 128)

    def share_when(core, half):
        pl.when(c == core)(lambda: share(half))

    share_when(0, 1)
    share_when(1, 0)

    axis_at = dict(x=x, y=y, z=z)
    axis_peers = dict(x=X_PEERS, y=Y_PEERS, z=Z_PEERS)

    class Chunk:
        def __init__(self, o, n, first, second, last, land1, sum1, land2, sum2, land3):
            self.o, self.n = o, n
            self.first, self.second, self.last = first, second, last
            self.land1, self.sum1, self.land2, self.sum2, self.land3 = land1, sum1, land2, sum2, land3
            self.wide = second if first == "x" else first
            self.flying = []

        def line(self, ref, start, along, index):
            block = (pl.ds(start, self.n),)
            return ref.at[block + ((index,) if along == "x" else (slice(None), index))]

        def go(self, pairs):
            self.flying = [copies.start(source, target, device) for source, target, device in pairs]

        def land(self):
            for copy in self.flying[::-1]:
                copy.wait()

        def targets(self, axis):
            where = AXES.index(axis)
            return [(i, peer(**o)[where], peer(**o)) for i, o in enumerate(axis_peers[axis])]

        def core_out(self):
            theirs = m.at[pl.ds(5 * (1 - c) + self.o, self.n)]
            self.go([(theirs, cl.at[pl.ds(self.o, self.n)], sibling)])

        def first_out(self):
            self.land()
            span = pl.ds(self.o, self.n)
            a1[span] = m[pl.ds(5 * c + self.o, self.n)] + cl[span]
            self.go([
                (self.line(a1, self.o, self.first, at), self.land1.at[i], device)
                for i, at, device in self.targets(self.first)
            ])

        def second_out(self):
            self.land()
            total = self.line(a1, self.o, self.first, axis_at[self.first])[...]
            for i in range(len(axis_peers[self.first])):
                total = total + self.land1[i]
            self.sum1[...] = total
            self.go([
                (self.sum1.at[:, at], self.land2.at[i], device)
                for i, at, device in self.targets(self.second)
            ])

        def last_out(self):
            self.land()
            total = self.sum1[:, axis_at[self.second]]
            for i in range(len(axis_peers[self.second])):
                total = total + self.land2[i]
            self.sum2[...] = total
            here = self.land3.at[axis_at[self.last]]
            here[...] = total
            self.go([(self.sum2, here, device) for _, _, device in self.targets(self.last)])

        def second_back(self):
            self.land()
            total = self.land3[0]
            for i in range(1, 8):
                total = total + self.land3[i]
            block = f.at[pl.ds(5 * c + self.o, self.n), x, axis_at[self.wide]]
            block[...] = total
            self.go([(block, block, device) for _, _, device in self.targets(self.second)])

        def first_back(self):
            self.land()
            block = self.line(f, 5 * c + self.o, self.first, axis_at[self.first])
            self.go([(block, block, device) for _, _, device in self.targets(self.first)])

        def core_back(self):
            if self.first != "x":
                self.land()
                block = f.at[pl.ds(5 * c + self.o, self.n)]
                self.go([(block, block, sibling)])
                return
            sent = self.flying
            block = self.line(f, 5 * c + self.o, "x", x)
            pairs = [copies.start(block, block, sibling)]
            for copy, o in list(zip(sent, X_PEERS))[::-1]:
                copy.wait_recv()
                block = self.line(f, 5 * c + self.o, "x", lax.rem(x + 4 - o["x"], 4))
                pairs.append(copies.start(block, block, sibling))
            for copy in sent:
                copy.wait_send()
            self.flying = pairs

    cx1 = Chunk(0, 2, "x", "z", "y", lx1, sx1, lx2, sx2, lx3)
    cx2 = Chunk(2, 1, "x", "z", "y", mx1, nx1, mx2, nx2, mx3)
    cz = Chunk(3, 1, "z", "x", "y", lz1, sz1, lz2, sz2, lz3)
    cy = Chunk(4, 1, "y", "x", "z", ly1, sy1, ly2, sy2, ly3)

    def begin_block():
        h = [pa[...], pb[...]]
        a[...] = transposed_kernel(px[...], px[...], row_norms(px[...])) - product(h, h, (1, 1), 2)
        row = lax.broadcasted_iota(jnp.int32, (B, B), 0)
        column = lax.broadcasted_iota(jnp.int32, (B, B), 1)
        xi[...] = jnp.where(row == column, 1.0, 0.0)

    def columns_of(i):
        flipped = product(split(xi[...], 3), split(rt[i], 3), (1, 0), 3)
        columns_out[i * 256 : (i + 1) * 256, :] = flipped.T

    for chunk in (cz, cy, cx1, cx2):
        chunk.core_out()
    share_when(0, 0)
    share_when(1, 1)
    for chunk in (cz, cy, cx1, cx2):
        chunk.first_out()
    begin_block()
    eliminate(0, 5, a, xi)
    for chunk in (cx1, cz, cy, cx2):
        chunk.second_out()
    eliminate(5, 8, a, xi)
    for chunk in (cz, cy, cx1, cx2):
        chunk.last_out()
    eliminate(8, 16, a, xi)
    for chunk in (cz, cy, cx1, cx2):
        chunk.second_back()
    columns_of(0)
    for chunk in (cz, cy, cx1, cx2):
        chunk.first_back()
    columns_of(1)
    for chunk in (cz, cy, cx1, cx2):
        chunk.core_back()

    inverse = split(xi[...], 3)
    scaled = 1.0 / (512 * 512)

    def applied(*blocks):
        total = jnp.concatenate([f[k].reshape(B, 128) for k in blocks], axis=1)
        return product(inverse, split(total, 3), (1, 0), 3)

    cz.land()
    cy.land()
    gram_out[:, 3 * 128 : 5 * 128] = scaled * applied(3, 4)
    gram_out[:, R:] = scaled * product(split(applied(8, 9), 3), inverse, (1, 1), 3)
    cx1.land()
    gram_out[:, :256] = scaled * applied(0, 1)
    gram_out[:, 5 * 128 : 7 * 128] = scaled * applied(5, 6)
    cx2.land()
    last = scaled * applied(2, 7)
    gram_out[:, 2 * 128 : 3 * 128] = last[:, :128]
    gram_out[:, 7 * 128 : 8 * 128] = last[:, 128:]


def sum_buffers(n, first, second):
    shapes = [
        (first, n, second, 8, 128),
        (n, second, 8, 128),
        (second - 1, n, 8, 128),
        (n, 8, 128),
        (8, n, 8, 128),
    ]
    return [pltpu.VMEM(shape, jnp.float32) for shape in shapes]


def run(features, factor, ip_weights, pivot_owner, pivot_position):
    count = 64 + 16 + 4 * 32
    vmem = pl.BlockSpec(memory_space=pltpu.VMEM)
    hbm = pl.BlockSpec(memory_space=pltpu.HBM)
    f32, bf16, i16 = jnp.float32, jnp.bfloat16, jnp.int16
    results = pl.pallas_call(
        whole_kernel,
        out_shape=(
            pltpu.VMEM((512, B), f32),
            pltpu.VMEM((B, R + B), f32),
        ),
        in_specs=[hbm] * 5,
        out_specs=(vmem, vmem),
        scratch_shapes=[
            pltpu.VMEM((1, B), jnp.int32),
            pltpu.VMEM((1, B), jnp.int32),
            pltpu.VMEM((2, 1, 256), f32),
            pltpu.VMEM((512, F), bf16),
            pltpu.VMEM((512, R), f32),
            pltpu.VMEM((512, R), bf16),
            pltpu.VMEM((512, R), bf16),
            pltpu.VMEM((1, 512), f32),
            pltpu.VMEM((B, 128), jnp.int32),
            pltpu.VMEM((16, 128), bf16),
            pltpu.VMEM((32, 128), i16),
            pltpu.VMEM((8, 16, 128), bf16),
            pltpu.VMEM((8, 32, 128), i16),
            pltpu.VMEM((4, 2, 16, 128), bf16),
            pltpu.VMEM((4, 2, 2, 16, 128), i16),
            pltpu.VMEM((7, 16, 128), bf16),
            pltpu.VMEM((7, 2, 16, 128), i16),
            pltpu.VMEM((16, 128), bf16),
            pltpu.VMEM((2, 16, 128), i16),
            pltpu.VMEM((7, 16, 128), bf16),
            pltpu.VMEM((7, 2, 16, 128), i16),
            pltpu.VMEM((2, 8, 4, 16, 128), bf16),
            pltpu.VMEM((2, 4, 8, 2, 16, 128), i16),
            pltpu.VMEM((B, F), bf16),
            pltpu.VMEM((B, R), bf16),
            pltpu.VMEM((B, R), bf16),
            pltpu.VMEM((2, B, 256), f32),
            pltpu.VMEM((B, 512), bf16),
            pltpu.VMEM((B, 512), bf16),
            pltpu.VMEM((B, 512), bf16),
            pltpu.VMEM((B, 512), bf16),
            pltpu.VMEM((10, 4, 8, 8, 128), f32),
            pltpu.VMEM((B, B), f32),
            pltpu.VMEM((B, B), f32),
            pltpu.VMEM((10, 4, 8, 8, 128), f32),
            pltpu.VMEM((5, 4, 8, 8, 128), f32),
            pltpu.VMEM((5, 4, 8, 8, 128), f32),
            *sum_buffers(2, 3, 8),
            *sum_buffers(1, 3, 8),
            *sum_buffers(1, 7, 4),
            *sum_buffers(1, 7, 4),
            pltpu.SemaphoreType.DMA((8,)),
            pltpu.SemaphoreType.DMA((count,)),
            pltpu.SemaphoreType.DMA((count,)),
        ],
        compiler_params=pltpu.CompilerParams(
            collective_id=0, has_side_effects=True, vmem_limit_bytes=48 * 2**20
        ),
    )(
        *(pltpu.with_memory_space_constraint(v, pltpu.HBM) for v in (
            pivot_owner.reshape(1, B), pivot_position.reshape(1, B), ip_weights.reshape(2, 1, 256), features, factor)),
    )
    vmem = pl.BlockSpec(memory_space=pltpu.VMEM)
    return pl.pallas_call(
        write_kernel,
        out_shape=(pltpu.HBM((512, B), f32), pltpu.HBM((B, R + B), f32)),
        in_specs=[vmem, vmem],
        out_specs=(hbm, hbm),
        scratch_shapes=[pltpu.SemaphoreType.DMA((3,))],
        compiler_params=pltpu.CompilerParams(vmem_limit_bytes=2**20),
    )(*results)


def write_kernel(columns, gram, columns_out, gram_out, sem):
    copies = [
        pltpu.make_async_copy(columns, columns_out, sem.at[0]),
        pltpu.make_async_copy(gram.at[pl.ds(0, 128)], gram_out.at[pl.ds(0, 128)], sem.at[1]),
        pltpu.make_async_copy(gram.at[pl.ds(128, 128)], gram_out.at[pl.ds(128, 128)], sem.at[2]),
    ]
    for copy in copies:
        copy.start()
    for copy in copies:
        copy.wait()


def solution(mesh):
    torus = Mesh(mesh.devices.reshape(4, 8, 2, 8), AXES)
    in_specs = (P(AXES, None), P(AXES, None), P(AXES), P(), P())
    out_specs = (P(AXES, None), P())
    return jax.shard_map(run, mesh=torus, in_specs=in_specs, out_specs=out_specs, check_vma=False)
```

```python
import jax
import jax.numpy as jnp
from jax import lax
from jax.experimental import pallas as pl
from jax.experimental.pallas import tpu as pltpu
from jax.sharding import Mesh
from jax.sharding import PartitionSpec as P

MESH = pl.DeviceIdType.MESH
AXES = ("x", "z", "c", "y")
SIZES = {"x": 4, "z": 8, "c": 2, "y": 8}
F = 512
R = 1024
B = 256
H_SCALE = 2.0**20


def coord(axis):
    return lax.axis_index(axis)


def peer(**offsets):
    return tuple(
        lax.rem(coord(a) + offsets[a] % SIZES[a], SIZES[a]) if a in offsets else coord(a) for a in AXES
    )


class Copies:
    def __init__(self, send_sem, recv_sem):
        self.send_sem, self.recv_sem, self.used = send_sem, recv_sem, 0

    def start(self, src, dst, device):
        copy = pltpu.make_async_remote_copy(
            src_ref=src,
            dst_ref=dst,
            send_sem=self.send_sem.at[self.used],
            recv_sem=self.recv_sem.at[self.used],
            device_id=device,
            device_id_type=MESH,
        )
        self.used += 1
        copy.start()
        return copy


def greet(peers):
    barrier = pltpu.get_barrier_semaphore()
    for device in peers:
        pl.semaphore_signal(barrier, inc=1, device_id=device, device_id_type=MESH)
    return lambda: pl.semaphore_wait(barrier, len(peers))


X_PEERS = [dict(x=d) for d in (2, 1, 3)]
Y_PEERS = [dict(y=d) for d in (4, 3, 5, 2, 6, 1, 7)]
Z_PEERS = [dict(z=d) for d in (4, 3, 5, 2, 6, 1, 7)]
XC_PEERS = [dict(x=d, c=e) for d in (2, 1, 3, 0) for e in (1, 0) if (d, e) != (0, 0)]
Z_ORDER = [dict(z=d) for d in (1, 7, 2, 6, 3, 5, 4)]
CORE = dict(c=1)
Z_GROUPS = ((0, 5), (5, 3))


W = 16


def split(values, count):
    out = []
    for _ in range(count - 1):
        part = values.astype(jnp.bfloat16)
        out.append(part)
        values = values - part.astype(jnp.float32)
    return out + [values.astype(jnp.bfloat16)]


def product(left, right, dims, count):
    order = {2: ((0, 0), (0, 1), (1, 0)), 3: ((0, 0), (0, 1), (1, 0), (0, 2), (2, 0), (1, 1))}[count]
    lhs = jnp.concatenate([left[i] for i, _ in order], axis=dims[0])
    rhs = jnp.concatenate([right[j] for _, j in order], axis=dims[1])
    return lax.dot_general(
        lhs, rhs, (((dims[0],), (dims[1],)), ((), ())), preferred_element_type=jnp.float32
    )


def row_norms(samples):
    ones = jnp.ones((8, F), jnp.bfloat16)
    norms = sum(
        lax.dot_general(ones, s, (((1,), (1,)), ((), ())), preferred_element_type=jnp.float32)
        for s in split(jnp.square(samples.astype(jnp.float32)), 2)
    )
    return norms[0:1]


def transposed_kernel(pivots, samples, norms):
    cross = lax.dot_general(
        pivots, samples, (((1,), (1,)), ((), ())), preferred_element_type=jnp.float32
    )
    pivot_norms = jnp.sum(jnp.square(pivots.astype(jnp.float32)), axis=1, keepdims=True)
    distance = pivot_norms + norms - 2.0 * cross
    quarter = jnp.exp(-(0.25 / F) * distance)
    half = quarter * quarter
    return 0.5 * quarter + 0.3 * half + 0.2 * (half * half)


def pivot_panel(p, base, a, xi):
    first = pl.multiple_of(p * W, W)
    rows = pl.ds(first, W)
    lanes = B - base
    s = a[rows, base:]
    xs = xi[rows, :]
    sub = lax.broadcasted_iota(jnp.int32, (W, 1), 0)
    lane = lax.broadcasted_iota(jnp.int32, (W, lanes), 1) + base
    columns = [
        jnp.sum(jnp.where(lane == first + j, s, 0.0), axis=1, keepdims=True) for j in range(W)
    ]
    pivots = jnp.ones((W, 1), jnp.float32)
    for j in range(W):
        pivot = columns[j][j : j + 1]
        factor = jnp.where(sub > j, columns[j] * (1.0 / pivot), 0.0)
        for k in range(j + 1, W):
            columns[k] = columns[k] - factor * columns[k][j : j + 1]
        s = s - factor * s[j : j + 1]
        xs = xs - factor * xs[j : j + 1]
        pivots = jnp.where(sub == j, pivot, pivots)
    scale = lax.rsqrt(pivots)
    xs = xs * scale
    later = jnp.where(lane >= first + W, s * scale, 0.0)
    update = product(
        split(later, 3), split(jnp.concatenate([later, xs], axis=1), 3), (0, 0), 3
    )
    a[base:, base:] = a[base:, base:] - update[:, :lanes]
    xi[base:, :] = xi[base:, :] - update[:, lanes:]
    xi[rows, :] = xs


def eliminate(first, last, a, xi):
    base = 0 if last * W <= B // 2 else B // 2

    def step(p, carry):
        pivot_panel(p, base, a, xi)
        return carry

    lax.fori_loop(first, last, step, 0)


def code_parts(codes):
    codes = codes.astype(jnp.int32)
    high = (codes + 128) >> 8
    return high.astype(jnp.float32), (codes - high * 256).astype(jnp.float32)


def whole_kernel(
    owner_hbm, position_hbm, weights_hbm, features_hbm, factor_hbm, columns_out, gram_out,
    owner, position, weights, features, factor, factor_hi, factor_lo, norms, table,
    sx, sh, rx, rh, tx, th, ax, ah, bx, bh, yx, yh, fx, fh,
    px, pa, pb, rt, rest_hi, rest_lo, weighted_hi, weighted_lo, m, a, xi, f, cl, a1,
    lx1, sx1, lx2, sx2, lx3, mx1, nx1, mx2, nx2, mx3, lz1, sz1, lz2, sz2, lz3, ly1, sy1, ly2, sy2, ly3,
    load_sem, send_sem, recv_sem,
):
    x, z, c, y = (coord(axis) for axis in AXES)
    copies = Copies(send_sem, recv_sem)
    wait_for_all = greet([peer(**o) for o in Z_PEERS + Y_PEERS + XC_PEERS])
    small = [
        pltpu.make_async_copy(source, target, load_sem.at[5 + i])
        for i, (source, target) in enumerate(
            ((owner_hbm, owner), (position_hbm, position), (weights_hbm, weights))
        )
    ]
    for load in small:
        load.start()
    load_x = pltpu.make_async_copy(features_hbm, features, load_sem.at[0])
    load_x.start()
    loads = []
    for i in range(4):
        rows = pl.ds(i * 128, 128)
        loads.append(
            pltpu.make_async_copy(factor_hbm.at[rows], factor.at[rows], load_sem.at[1 + i])
        )
        loads[i].start()
    sibling = peer(**CORE)

    me = ((x * 8 + z) * 2 + c) * 8 + y
    for load in small:
        load.wait()
    row_owner = owner[...]
    col_owner = jnp.broadcast_to(row_owner.astype(jnp.float32), (B, B)).T.astype(jnp.int32)
    i_row = lax.broadcasted_iota(jnp.int32, (B, B), 0)
    i_col = lax.broadcasted_iota(jnp.int32, (B, B), 1)
    same = col_owner == row_owner
    row_rank = jnp.sum(jnp.where(same & (i_row < i_col), 1.0, 0.0), axis=0, keepdims=True)
    col_rank = jnp.sum(jnp.where(same & (i_col < i_row), 1.0, 0.0), axis=1, keepdims=True)
    near = col_owner[:, :128] // 128 == x
    near = near & (col_owner[:, :128] % 8 == y) & ((col_owner[:, :128] // 8) % 2 == c)
    place = (col_owner[:, :128] // 16) % 8 * 4 + col_rank.astype(jnp.int32)
    table[...] = jnp.where(near, place, -64)

    order = row_rank.astype(jnp.int32)
    spots = [
        jnp.sum(jnp.where((row_owner == me) & (order == s), position[...], 0)) for s in range(4)
    ]
    slot = lax.broadcasted_iota(jnp.int32, (16, 512), 0) // 4
    lane = lax.broadcasted_iota(jnp.int32, (16, 512), 1)
    wanted = jnp.where(slot == 0, spots[0], jnp.where(slot == 1, spots[1], jnp.where(slot == 2, spots[2], spots[3])))
    pick = jnp.where(lane == wanted, 1.0, 0.0).astype(jnp.bfloat16)
    load_x.wait()
    rows_x = jnp.dot(pick, features[...], preferred_element_type=jnp.float32)
    block_x = lax.broadcasted_iota(jnp.int32, (16, 128), 0) % 4
    sx[...] = sum(
        jnp.where(block_x == b, rows_x[:, b * 128 : b * 128 + 128], 0.0) for b in range(4)
    ).astype(jnp.bfloat16)
    for load in loads:
        load.wait()
    rows_h = [factor[pl.ds(spot, 1), :] for spot in spots]
    own_h = jnp.concatenate(
        [row[:, b * 128 : b * 128 + 128] for row in rows_h for b in range(8)], axis=0
    )
    sh[...] = jnp.round(own_h * H_SCALE).astype(jnp.int32).astype(jnp.int16)

    wait_for_all()
    pending = []
    for o in Z_PEERS:
        pending.append(copies.start(sx, rx.at[z], peer(**o)))
        pending.append(copies.start(sh, rh.at[z], peer(**o)))
    rx[z] = sx[...]
    rh[z] = sh[...]

    def cut(i, carry):
        rows = pl.ds(pl.multiple_of(i * 64, 64), 64)
        factor_hi[rows, :], factor_lo[rows, :] = split(factor[rows, :], 2)
        return carry

    lax.fori_loop(0, 8, cut, 0)
    norms[...] = row_norms(features[...])
    target = table[pl.ds(pl.multiple_of(z * 32, 32), 32), :][:, :1]
    halves = [target[:16], target[16:]]
    target_x = jnp.concatenate([target * 4 + b for b in range(4)], axis=0)
    target_h = jnp.concatenate(
        [half * 8 + (2 * b + j) for b in range(4) for half in halves for j in range(2)], axis=0
    )
    pick_x = jnp.where(
        lax.broadcasted_iota(jnp.int32, (128, 128), 1) == target_x, 1.0, 0.0
    ).astype(jnp.bfloat16)
    pick_h = jnp.where(
        lax.broadcasted_iota(jnp.int32, (256, 256), 1) == target_h, 1.0, 0.0
    ).astype(jnp.bfloat16)
    for copy in pending[::-1]:
        copy.wait()
    tx[...] = jnp.dot(
        pick_x, rx[...].reshape(8 * 16, 128), preferred_element_type=jnp.float32
    ).astype(jnp.bfloat16).reshape(4, 2, 16, 128)
    high, low = code_parts(rh[...].reshape(8 * 32, 128))
    picked = 256.0 * jnp.dot(
        pick_h, high.astype(jnp.bfloat16), preferred_element_type=jnp.float32
    ) + jnp.dot(pick_h, low.astype(jnp.bfloat16), preferred_element_type=jnp.float32)
    th[...] = picked.astype(jnp.int32).astype(jnp.int16).reshape(4, 2, 2, 16, 128)

    pending = []
    for i, o in enumerate(XC_PEERS):
        device = peer(**o)
        pending.append(copies.start(tx.at[device[0], device[2]], ax.at[i], device))
        pending.append(copies.start(th.at[device[0], device[2]], ah.at[i], device))
    for copy in pending[::-1]:
        copy.wait()
    total_x = tx[x, c].astype(jnp.float32)
    total_h = th[x, c].astype(jnp.int32)
    for i in range(7):
        total_x = total_x + ax[i].astype(jnp.float32)
        total_h = total_h + ah[i].astype(jnp.int32)
    bx[...] = total_x.astype(jnp.bfloat16)
    bh[...] = total_h.astype(jnp.int16)

    pending = []
    for i, o in enumerate(Y_PEERS):
        pending.append(copies.start(bx, yx.at[i], peer(**o)))
        pending.append(copies.start(bh, yh.at[i], peer(**o)))
    for copy in pending[::-1]:
        copy.wait()
    for i in range(7):
        total_x = total_x + yx[i].astype(jnp.float32)
        total_h = total_h + yh[i].astype(jnp.int32)
    fx[c, 0, x] = total_x.astype(jnp.bfloat16)
    fh[c, x, 0] = total_h.astype(jnp.int16)

    z_first = [
        copies.start(fh.at[c, x, 0], fh.at[c, x, 7 - i], peer(**o)) for i, o in enumerate(Z_ORDER[::-1])
    ][::-1]
    x_first = [copies.start(fx.at[c, 0, x], fx.at[c, 0, x], peer(**o)) for o in X_PEERS]
    for copy in x_first:
        copy.wait_recv()
    z_second = [
        copies.start(fx.at[c, 0], fx.at[c, 7 - i], peer(**o)) for i, o in enumerate(Z_ORDER[::-1])
    ][::-1]
    x_second, across = [], []
    for first, size in Z_GROUPS:
        for i in range(max(first, 1), first + size):
            z_first[i - 1].wait_recv()
        part = fh.at[c, x, pl.ds(first, size)]
        for o in X_PEERS:
            x_second.append(copies.start(part, part, peer(**o)))
        across.append(copies.start(part, part, sibling))
    for first, size in Z_GROUPS:
        for i in range(max(first, 1), first + size):
            z_second[i - 1].wait_recv()
        part = fx.at[c, pl.ds(first, size)]
        across.append(copies.start(part, part, sibling))
    for g, (first, size) in enumerate(Z_GROUPS):
        for i, o in list(enumerate(X_PEERS))[::-1]:
            source = lax.rem(x + 4 - o["x"], 4)
            part = fh.at[c, source, pl.ds(first, size)]
            x_second[g * 3 + i].wait_recv()
            across.append(copies.start(part, part, sibling))

    def unpack(core):
        def step(i, carry):
            odd = i % 2
            back = odd * ((i + 1) // 2) + (1 - odd) * (8 - i // 2)
            rows = pl.ds(pl.multiple_of((((z + 8 - back) % 8) * 2 + core) * 16, 16), 16)
            for xb in range(4):
                px[rows, xb * 128 : xb * 128 + 128] = fx[core, i, xb]
                for j in range(2):
                    high, low = code_parts(fh[core, xb, i, j])
                    at = (xb * 2 + j) * 128
                    pa[rows, at : at + 128] = (high * (256.0 / H_SCALE)).astype(jnp.bfloat16)
                    pb[rows, at : at + 128] = (low * (1.0 / H_SCALE)).astype(jnp.bfloat16)
            return carry

        lax.fori_loop(0, 8, step, 0)

    unpack(c)
    for copy in x_first + z_first + z_second + x_second:
        copy.wait_send()
    for copy in across:
        copy.wait()
    unpack(1 - c)

    def local(i, carry):
        span = pl.ds(pl.multiple_of(i * 256, 256), 256)
        h = [factor_hi[span, :], factor_lo[span, :]]
        residual = transposed_kernel(px[...], features[span, :], norms[:, span]) - product(
            [pa[...], pb[...]], h, (1, 1), 2
        )
        rt[i] = residual
        rest_hi[:, span], rest_lo[:, span] = split(residual, 2)
        weighted_hi[:, span], weighted_lo[:, span] = split(residual * weights[i], 2)
        return carry

    lax.fori_loop(0, 2, local, 0)

    def share(half):
        weighted = [weighted_hi[...], weighted_lo[...]]
        lanes = slice(0, 640) if half == 0 else slice(640, R)
        values = product(weighted, [factor_hi[:, lanes], factor_lo[:, lanes]], (1, 0), 2)
        if half == 1:
            right = product(weighted, [rest_hi[...], rest_lo[...]], (1, 1), 2)
            values = jnp.concatenate([values, right], axis=1)
        for k in range(5):
            m[5 * half + k] = values[:, k * 128 : k * 128 + 128].reshape(4, 8, 8, 128)

    def share_when(core, half):
        pl.when(c == core)(lambda: share(half))

    share_when(0, 1)
    share_when(1, 0)

    axis_at = dict(x=x, y=y, z=z)
    axis_peers = dict(x=X_PEERS, y=Y_PEERS, z=Z_PEERS)

    class Chunk:
        def __init__(self, o, n, first, second, last, land1, sum1, land2, sum2, land3):
            self.o, self.n = o, n
            self.first, self.second, self.last = first, second, last
            self.land1, self.sum1, self.land2, self.sum2, self.land3 = land1, sum1, land2, sum2, land3
            self.wide = second if first == "x" else first
            self.flying = []

        def line(self, ref, start, along, index):
            block = (pl.ds(start, self.n),)
            return ref.at[block + ((index,) if along == "x" else (slice(None), index))]

        def go(self, pairs):
            self.flying = [copies.start(source, target, device) for source, target, device in pairs]

        def land(self):
            for copy in self.flying[::-1]:
                copy.wait()

        def targets(self, axis):
            where = AXES.index(axis)
            return [(i, peer(**o)[where], peer(**o)) for i, o in enumerate(axis_peers[axis])]

        def core_out(self):
            theirs = m.at[pl.ds(5 * (1 - c) + self.o, self.n)]
            self.go([(theirs, cl.at[pl.ds(self.o, self.n)], sibling)])

        def first_out(self):
            self.land()
            span = pl.ds(self.o, self.n)
            a1[span] = m[pl.ds(5 * c + self.o, self.n)] + cl[span]
            self.go([
                (self.line(a1, self.o, self.first, at), self.land1.at[i], device)
                for i, at, device in self.targets(self.first)
            ])

        def second_out(self):
            self.land()
            total = self.line(a1, self.o, self.first, axis_at[self.first])[...]
            for i in range(len(axis_peers[self.first])):
                total = total + self.land1[i]
            self.sum1[...] = total
            self.go([
                (self.sum1.at[:, at], self.land2.at[i], device)
                for i, at, device in self.targets(self.second)
            ])

        def last_out(self):
            self.land()
            total = self.sum1[:, axis_at[self.second]]
            for i in range(len(axis_peers[self.second])):
                total = total + self.land2[i]
            self.sum2[...] = total
            here = self.land3.at[axis_at[self.last]]
            here[...] = total
            self.go([(self.sum2, here, device) for _, _, device in self.targets(self.last)])

        def second_back(self):
            self.land()
            total = self.land3[0]
            for i in range(1, 8):
                total = total + self.land3[i]
            block = f.at[pl.ds(5 * c + self.o, self.n), x, axis_at[self.wide]]
            block[...] = total
            self.go([(block, block, device) for _, _, device in self.targets(self.second)])

        def first_back(self):
            self.land()
            block = self.line(f, 5 * c + self.o, self.first, axis_at[self.first])
            self.go([(block, block, device) for _, _, device in self.targets(self.first)])

        def core_back(self):
            if self.first != "x":
                self.land()
                block = f.at[pl.ds(5 * c + self.o, self.n)]
                self.go([(block, block, sibling)])
                return
            sent = self.flying
            block = self.line(f, 5 * c + self.o, "x", x)
            pairs = [copies.start(block, block, sibling)]
            for copy, o in list(zip(sent, X_PEERS))[::-1]:
                copy.wait_recv()
                block = self.line(f, 5 * c + self.o, "x", lax.rem(x + 4 - o["x"], 4))
                pairs.append(copies.start(block, block, sibling))
            for copy in sent:
                copy.wait_send()
            self.flying = pairs

    cx1 = Chunk(0, 2, "x", "z", "y", lx1, sx1, lx2, sx2, lx3)
    cx2 = Chunk(2, 1, "x", "z", "y", mx1, nx1, mx2, nx2, mx3)
    cz = Chunk(3, 1, "z", "x", "y", lz1, sz1, lz2, sz2, lz3)
    cy = Chunk(4, 1, "y", "x", "z", ly1, sy1, ly2, sy2, ly3)

    def begin_block():
        h = [pa[...], pb[...]]
        a[...] = transposed_kernel(px[...], px[...], row_norms(px[...])) - product(h, h, (1, 1), 2)
        row = lax.broadcasted_iota(jnp.int32, (B, B), 0)
        column = lax.broadcasted_iota(jnp.int32, (B, B), 1)
        xi[...] = jnp.where(row == column, 1.0, 0.0)

    def columns_of(i):
        flipped = product(split(xi[...], 3), split(rt[i], 3), (1, 0), 3)
        columns_out[i * 256 : (i + 1) * 256, :] = flipped.T

    for chunk in (cz, cy, cx1, cx2):
        chunk.core_out()
    share_when(0, 0)
    share_when(1, 1)
    for chunk in (cz, cy, cx1, cx2):
        chunk.first_out()
    begin_block()
    eliminate(0, 5, a, xi)
    for chunk in (cx1, cz, cy, cx2):
        chunk.second_out()
    eliminate(5, 8, a, xi)
    for chunk in (cz, cy, cx1, cx2):
        chunk.last_out()
    eliminate(8, 16, a, xi)
    for chunk in (cz, cy, cx1, cx2):
        chunk.second_back()
    columns_of(0)
    for chunk in (cz, cy, cx1, cx2):
        chunk.first_back()
    columns_of(1)
    for chunk in (cz, cy, cx1, cx2):
        chunk.core_back()

    inverse = split(xi[...], 3)
    scaled = 1.0 / (512 * 512)

    def applied(*blocks):
        total = jnp.concatenate([f[k].reshape(B, 128) for k in blocks], axis=1)
        return product(inverse, split(total, 3), (1, 0), 3)

    cz.land()
    cy.land()
    gram_out[:, 3 * 128 : 5 * 128] = scaled * applied(3, 4)
    gram_out[:, R:] = scaled * product(split(applied(8, 9), 3), inverse, (1, 1), 3)
    cx1.land()
    gram_out[:, :256] = scaled * applied(0, 1)
    gram_out[:, 5 * 128 : 7 * 128] = scaled * applied(5, 6)
    cx2.land()
    last = scaled * applied(2, 7)
    gram_out[:, 2 * 128 : 3 * 128] = last[:, :128]
    gram_out[:, 7 * 128 : 8 * 128] = last[:, 128:]


def sum_buffers(n, first, second):
    shapes = [
        (first, n, second, 8, 128),
        (n, second, 8, 128),
        (second - 1, n, 8, 128),
        (n, 8, 128),
        (8, n, 8, 128),
    ]
    return [pltpu.VMEM(shape, jnp.float32) for shape in shapes]


def run(features, factor, ip_weights, pivot_owner, pivot_position):
    count = 64 + 16 + 4 * 32
    vmem = pl.BlockSpec(memory_space=pltpu.VMEM)
    hbm = pl.BlockSpec(memory_space=pltpu.HBM)
    f32, bf16, i16 = jnp.float32, jnp.bfloat16, jnp.int16
    results = pl.pallas_call(
        whole_kernel,
        out_shape=(
            pltpu.VMEM((512, B), f32),
            pltpu.VMEM((B, R + B), f32),
        ),
        in_specs=[hbm] * 5,
        out_specs=(vmem, vmem),
        scratch_shapes=[
            pltpu.VMEM((1, B), jnp.int32),
            pltpu.VMEM((1, B), jnp.int32),
            pltpu.VMEM((2, 1, 256), f32),
            pltpu.VMEM((512, F), bf16),
            pltpu.VMEM((512, R), f32),
            pltpu.VMEM((512, R), bf16),
            pltpu.VMEM((512, R), bf16),
            pltpu.VMEM((1, 512), f32),
            pltpu.VMEM((B, 128), jnp.int32),
            pltpu.VMEM((16, 128), bf16),
            pltpu.VMEM((32, 128), i16),
            pltpu.VMEM((8, 16, 128), bf16),
            pltpu.VMEM((8, 32, 128), i16),
            pltpu.VMEM((4, 2, 16, 128), bf16),
            pltpu.VMEM((4, 2, 2, 16, 128), i16),
            pltpu.VMEM((7, 16, 128), bf16),
            pltpu.VMEM((7, 2, 16, 128), i16),
            pltpu.VMEM((16, 128), bf16),
            pltpu.VMEM((2, 16, 128), i16),
            pltpu.VMEM((7, 16, 128), bf16),
            pltpu.VMEM((7, 2, 16, 128), i16),
            pltpu.VMEM((2, 8, 4, 16, 128), bf16),
            pltpu.VMEM((2, 4, 8, 2, 16, 128), i16),
            pltpu.VMEM((B, F), bf16),
            pltpu.VMEM((B, R), bf16),
            pltpu.VMEM((B, R), bf16),
            pltpu.VMEM((2, B, 256), f32),
            pltpu.VMEM((B, 512), bf16),
            pltpu.VMEM((B, 512), bf16),
            pltpu.VMEM((B, 512), bf16),
            pltpu.VMEM((B, 512), bf16),
            pltpu.VMEM((10, 4, 8, 8, 128), f32),
            pltpu.VMEM((B, B), f32),
            pltpu.VMEM((B, B), f32),
            pltpu.VMEM((10, 4, 8, 8, 128), f32),
            pltpu.VMEM((5, 4, 8, 8, 128), f32),
            pltpu.VMEM((5, 4, 8, 8, 128), f32),
            *sum_buffers(2, 3, 8),
            *sum_buffers(1, 3, 8),
            *sum_buffers(1, 7, 4),
            *sum_buffers(1, 7, 4),
            pltpu.SemaphoreType.DMA((8,)),
            pltpu.SemaphoreType.DMA((count,)),
            pltpu.SemaphoreType.DMA((count,)),
        ],
        compiler_params=pltpu.CompilerParams(
            collective_id=0, has_side_effects=True, vmem_limit_bytes=48 * 2**20
        ),
    )(
        *(pltpu.with_memory_space_constraint(v, pltpu.HBM) for v in (
            pivot_owner.reshape(1, B), pivot_position.reshape(1, B), ip_weights.reshape(2, 1, 256), features, factor)),
    )
    vmem = pl.BlockSpec(memory_space=pltpu.VMEM)
    return pl.pallas_call(
        write_kernel,
        out_shape=(pltpu.HBM((512, B), f32), pltpu.HBM((B, R + B), f32)),
        in_specs=[vmem, vmem],
        out_specs=(hbm, hbm),
        scratch_shapes=[pltpu.SemaphoreType.DMA((3,))],
        compiler_params=pltpu.CompilerParams(vmem_limit_bytes=2**20),
    )(*results)


def write_kernel(columns, gram, columns_out, gram_out, sem):
    copies = [
        pltpu.make_async_copy(columns, columns_out, sem.at[0]),
        pltpu.make_async_copy(gram.at[pl.ds(0, 128)], gram_out.at[pl.ds(0, 128)], sem.at[1]),
        pltpu.make_async_copy(gram.at[pl.ds(128, 128)], gram_out.at[pl.ds(128, 128)], sem.at[2]),
    ]
    for copy in copies:
        copy.start()
    for copy in copies:
        copy.wait()


def solution(mesh):
    torus = Mesh(mesh.devices.reshape(4, 8, 2, 8), AXES)
    in_specs = (P(AXES, None), P(AXES, None), P(AXES), P(), P())
    out_specs = (P(AXES, None), P())
    return jax.shard_map(run, mesh=torus, in_specs=in_specs, out_specs=out_specs, check_vma=False)
```
